32 devices in a mesh: row: 8 (over z, x), col: 4 (over y, core).
Axes of the slice: x: 2, y: 2, z: 4, core: 2. Of those that a mesh axis runs over, the one named last changes fastest.
Arguments:
- vectors: bfloat16 [256, 16384], P('col', 'row'), may hold values from -6 to 6
- hblocks: bfloat16 [256, 12, 4096], P('row'), may hold values from -0.15625 to 0.15625
- counts: int32 [256], P('row'), may hold values from 3 to 12, as said below
- sources: int32 [256, 12], P('row'), may hold values from 0 to 47, as said below
- send_rows: int32 [128], P('row'), may hold values from 0 to 31
Outputs:
- filtered: bfloat16 [256, 16384], P('col', 'row')
- gram_matrix: float32 [256, 256], P(None, 'col')
- projected: float32 [256, 256], P(None, 'col')
The draws below stay inside these ranges and needn't reach their ends.
Inputs may be any that keep to these rules, and one draw needn't show every extreme that they name: Blocks 0 to counts[i] - 1 of block row i are live; the rows of every device include one with 12 live blocks. `sources`: entry 0 of block row i is i's own index within its device. On every device each slot value 32 + s, s below 16, stands exactly once, at block 1 or 2 of some row. `send_rows`: entries p * 16 + q * 2 + c name block rows of device p within it.
All inputs are finite; a program needn't handle non-finite values.
Results may differ from the reference program's by a relative error of at most 0.017.
Values may be sent and summed in bfloat16 or wider, within the bound.
A program may use at most 128 MiB of HBM per device.

```python
import jax
import jax.numpy as jnp
from jax import lax

B = 64
M = 256
K = 12
C = 2
RB = 32
NB = 256
SLOTS = 16
N = 16384
N_ROW = 8


def draw_counts(key, part):
    values = jax.random.randint(key, (NB,), 3, K + 1, dtype=jnp.int32)
    chosen_rows = jax.random.randint(jax.random.fold_in(key, 5), (NB // RB,), 0, RB, dtype=jnp.int32)
    return values.at[jnp.arange(NB // RB, dtype=jnp.int32) * RB + chosen_rows].set(K)


def draw_sources(key, part):
    devices = NB // RB

    def per_device(device):
        device_key = jax.random.fold_in(key, device)
        entries = jax.random.randint(jax.random.fold_in(device_key, 1), (RB, K), 0, RB, dtype=jnp.int32)
        entries = entries.at[:, 0].set(jnp.arange(RB, dtype=jnp.int32))
        shuffle = jax.random.permutation(jax.random.fold_in(device_key, 2), RB)
        positions = jnp.arange(SLOTS, dtype=jnp.int32)
        return entries.at[shuffle[positions % RB], 1 + positions // RB].set(RB + positions)
    return jax.vmap(per_device)(jnp.arange(devices, dtype=jnp.int32)).reshape(NB, K)


def touch_ends(values, own_key, low, largest):
    longest = values.shape.index(max(values.shape))
    spots = []
    for shift in (0, 1):
        where = [jax.random.randint(jax.random.fold_in(own_key, axis), (), 0, length) for axis, length in enumerate(values.shape)]
        where[longest] = (where[longest] + shift) % values.shape[longest]
        spots.append(tuple(where))
    return values.at[spots[0]].set(low).at[spots[1]].set(largest)


def block_scale(stream_key, dims, split, least, largest):
    gain = 1.0
    for position, parts in split:
        heights = jax.random.uniform(jax.random.fold_in(jax.random.fold_in(stream_key, 6), position), (parts,), jnp.float32, least / len(split), largest / len(split))
        gain = gain * jnp.repeat(jnp.exp(heights), dims[position] // parts).reshape((-1,) + (1,) * (len(dims) - 1 - position))
    return gain


def normal_values(rng, shape, width, bound, pieces=(), kind=jnp.bfloat16):
    gain = block_scale(rng, shape, pieces, -0.22, 0.18) if pieces else 1.0
    values = jax.random.normal(rng, shape, jnp.float32) * width * gain
    return jnp.minimum(jnp.maximum(values, -bound), bound).astype(kind)


def setup_inputs(seed: int = 0) -> dict:
    keys = jax.random.split(jax.random.key(seed), 6)
    vectors = normal_values(keys[0], (M, N), 1.0, 6.0, ((0, 4), (1, 8)))
    hblocks = normal_values(keys[1], (NB, K, B * B), (2 * K * B) ** -0.5, 0.15625, ((0, 8),))
    counts = draw_counts(jax.random.fold_in(keys[5], 71), 0)
    sources = draw_sources(jax.random.fold_in(keys[5], 71), 0)
    send_rows = touch_ends(jax.random.randint(keys[4], (N_ROW * SLOTS,), 0, RB), jax.random.fold_in(keys[4], 1), 0, RB - 1).astype(jnp.int32)
    return dict(vectors=vectors, hblocks=hblocks, counts=counts, sources=sources, send_rows=send_rows)


center_value = 0.25
half_width = 1.5


def column_blocks(sources, send_rows):
    row_index = jnp.arange(NB, dtype=jnp.int32)[:, None]
    owner_row = row_index // RB
    slot_index = jnp.maximum(sources - RB, 0)
    peer_index = slot_index // C
    within_peer = slot_index % C
    remote = peer_index * RB + send_rows[(peer_index * SLOTS + owner_row * C + within_peer).astype(jnp.int32)]
    return jnp.where(sources < RB, owner_row * RB + sources, remote).astype(jnp.int32)


def apply_operator(block_vectors, masked, gcol):
    def accumulate(group, accum):
        offset = (group * RB).astype(jnp.int32)
        group_blocks = lax.dynamic_slice_in_dim(masked, offset, RB, 0).astype(jnp.float32)
        group_columns = lax.dynamic_slice_in_dim(gcol, offset, RB, 0)
        group_vectors = lax.dynamic_slice_in_dim(block_vectors, offset, RB, 0).astype(jnp.float32)
        picked = block_vectors[group_columns].astype(jnp.float32)
        upper_part = jnp.einsum("ikmb,ikab->ima", picked, group_blocks, precision=lax.Precision.HIGHEST)
        mirror = jnp.einsum("ima,ikab->ikmb", group_vectors, group_blocks, precision=lax.Precision.HIGHEST)
        current = lax.dynamic_slice_in_dim(accum, offset, RB, 0)
        accum = lax.dynamic_update_slice_in_dim(accum, current + upper_part, offset, 0)
        return accum.at[group_columns.reshape(-1)].add(mirror.reshape(RB * K, M, B))
    return lax.fori_loop(0, NB // RB, accumulate, jnp.zeros((NB, M, B), jnp.float32))


def reference(vectors, hblocks, counts, sources, send_rows):
    gcol = column_blocks(sources, send_rows)
    live_mask = jnp.arange(K, dtype=jnp.int32)[None, :] < counts[:, None]
    masked = jnp.where(live_mask[:, :, None], hblocks, jnp.zeros((), hblocks.dtype)).reshape(NB, K, B, B)
    start_blocks = vectors.reshape(M, NB, B).transpose(1, 0, 2)
    start_float = start_blocks.astype(jnp.float32)
    first_image = apply_operator(start_blocks, masked, gcol)
    first_step = ((first_image - center_value * start_float) / half_width).astype(jnp.bfloat16)
    second_image = apply_operator(first_step, masked, gcol)
    second_step = (2.0 * (second_image - center_value * first_step.astype(jnp.float32)) / half_width - start_float).astype(jnp.bfloat16)
    image_blocks = apply_operator(second_step, masked, gcol).astype(jnp.bfloat16)
    filtered = second_step.transpose(1, 0, 2).reshape(M, NB * B)
    image_rows = image_blocks.transpose(1, 0, 2).reshape(M, NB * B)
    gram_matrix = jnp.dot(filtered, filtered.T, preferred_element_type=jnp.float32)
    projected = jnp.dot(filtered, image_rows.T, preferred_element_type=jnp.float32)
    return (filtered, gram_matrix, projected)
```

```python
import functools

import jax
import jax.numpy as jnp
from jax import lax
from jax.experimental import pallas as pl
from jax.experimental.pallas import tpu as pltpu
from jax.sharding import PartitionSpec as P

B = 64
K = 12
PAIR = 2 * B
TILE = 256

center_value = 0.25
half_width = 1.5

MESH = pl.DeviceIdType.MESH
NN = (((1,), (0,)), ((), ()))
NT = (((1,), (1,)), ((), ()))


def dot(a, b, dims):
    return lax.dot_general(a, b, dims, preferred_element_type=jnp.float32)


def filter_kernel(
    n_row, n_col, send_rows, mask, x0, u,
    filtered, gram, projected,
    step_one, stacked, total, blocks, spread, out_buf, in_buf, gathered,
    piece_out, piece_in, sum_out, sum_in,
    send_sem, recv_sem, col_send, col_recv, piece_send, piece_recv, sum_send, sum_recv,
):
    me = lax.axis_index("row")
    mine = lax.axis_index("col")
    cols, length = x0.shape
    pairs = length // PAIR
    slots = 2 * n_row

    barrier = pltpu.get_barrier_semaphore()
    for step in range(1, n_row):
        pl.semaphore_signal(barrier, inc=1, device_id={"row": lax.rem(me + step, n_row)}, device_id_type=MESH)
    for step in range(1, n_col):
        pl.semaphore_signal(barrier, inc=1, device_id={"col": lax.rem(mine + step, n_col)}, device_id_type=MESH)
    pl.semaphore_wait(barrier, n_row + n_col - 2)

    lane = lax.broadcasted_iota(jnp.int32, (cols, PAIR), 1)
    low = lane < B

    def columns(index, width):
        return pl.ds(pl.multiple_of(index * width, width), width)

    def both(values):
        turned = pltpu.roll(values, B, 1)
        return jnp.where(low, values, turned), jnp.where(low, turned, values)

    def keep_blocks(pair, values):
        first, second = both(values)
        blocks[2 * pair] = first.astype(jnp.bfloat16)
        blocks[2 * pair + 1] = second.astype(jnp.bfloat16)

    def start_body(pair, carry):
        keep_blocks(pair, x0[:, columns(pair, PAIR)].astype(jnp.float32))
        return carry

    lax.fori_loop(0, pairs, start_body, 0)

    def row_copy(phase, slot_here, slot_there, peer):
        return pltpu.make_async_remote_copy(
            src_ref=out_buf.at[phase, slot_here],
            dst_ref=in_buf.at[phase, slot_there],
            send_sem=send_sem.at[phase, slot_here],
            recv_sem=recv_sem.at[phase, slot_there],
            device_id={"row": peer},
            device_id_type=MESH,
        )

    def apply_operator(phase, source, finish):
        def gather_body(peer, carry):
            first = blocks[send_rows[2 * peer]].astype(jnp.float32)
            second = blocks[send_rows[2 * peer + 1]].astype(jnp.float32)
            out_buf[phase, peer, :, pl.ds(0, PAIR)] = jnp.where(low, first, second).astype(jnp.bfloat16)
            return carry

        lax.fori_loop(0, n_row, gather_body, 0)

        def mirror_body(tile, carry):
            here = pl.ds(pl.multiple_of(length + tile * TILE, TILE), TILE)
            product = dot(source[...], u[:, here], NN).astype(jnp.bfloat16)
            out_buf[phase, 2 * tile, :, pl.ds(PAIR, PAIR)] = product[:, :PAIR]
            out_buf[phase, 2 * tile + 1, :, pl.ds(PAIR, PAIR)] = product[:, PAIR:]
            return carry

        lax.fori_loop(0, n_row // 2, mirror_body, 0)
        for step in range(1, n_row):
            peer = lax.rem(me + step, n_row)
            row_copy(phase, peer, me, peer).start()
        in_buf[phase, me] = out_buf[phase, me]

        def local_body(tile, carry):
            here = columns(tile, TILE)
            total[:, here] = dot(source[...], u[:, here], NN) + dot(source[...], u[here, pl.ds(0, length)], NT)
            return carry

        lax.fori_loop(0, length // TILE, local_body, 0)
        for step in range(1, n_row):
            peer = lax.rem(me + step, n_row)
            row_copy(phase, peer, peer, peer).wait_recv()

        arrived = jnp.concatenate([in_buf[phase, peer, :, pl.ds(0, PAIR)] for peer in range(n_row)], 1)

        def remote_body(tile, carry):
            here = columns(tile, TILE)
            total[:, here] += dot(arrived, u[here, pl.ds(length, slots * B)], NT)
            return carry

        lax.fori_loop(0, length // TILE, remote_body, 0)

        def spread_body(peer, carry):
            first, second = both(in_buf[phase, peer, :, pl.ds(PAIR, PAIR)].astype(jnp.float32))
            spread[2 * peer] = first
            spread[2 * peer + 1] = second
            return carry

        lax.fori_loop(0, n_row, spread_body, 0)

        def finish_body(pair, carry):
            here = columns(pair, PAIR)
            value = total[:, here]
            for slot in range(slots):
                value = value + spread[slot] * mask[pl.ds(slot, 1), here]
            finish(pair, here, value)
            return carry

        lax.fori_loop(0, pairs, finish_body, 0)
        for step in range(1, n_row):
            peer = lax.rem(me + step, n_row)
            row_copy(phase, peer, me, peer).wait_send()

    def first_finish(pair, here, value):
        new = ((value - center_value * x0[:, here].astype(jnp.float32)) / half_width).astype(jnp.bfloat16)
        step_one[:, here] = new
        keep_blocks(pair, new.astype(jnp.float32))

    def second_finish(pair, here, value):
        old = step_one[:, here].astype(jnp.float32)
        new = (
            2.0 * (value - center_value * old) / half_width - x0[:, here].astype(jnp.float32)
        ).astype(jnp.bfloat16)
        stacked[pl.ds(0, cols), here] = new
        gathered[mine, :, here] = new
        filtered[:, here] = new
        keep_blocks(pair, new.astype(jnp.float32))

    def third_finish(pair, here, value):
        stacked[pl.ds(cols, cols), here] = value.astype(jnp.bfloat16)

    def col_copy(slot, peer):
        return pltpu.make_async_remote_copy(
            src_ref=gathered.at[mine],
            dst_ref=gathered.at[slot],
            send_sem=col_send.at[peer],
            recv_sem=col_recv.at[slot],
            device_id={"col": peer},
            device_id_type=MESH,
        )

    apply_operator(0, x0, first_finish)
    apply_operator(1, step_one, second_finish)
    for step in range(1, n_col):
        peer = lax.rem(mine + step, n_col)
        col_copy(mine, peer).start()
    apply_operator(2, stacked.at[pl.ds(0, cols)], third_finish)
    for step in range(1, n_col):
        peer = lax.rem(mine + step, n_col)
        col_copy(peer, peer).wait_recv()

    piece = n_col * cols // n_row

    for group in range(n_col):
        part = dot(gathered[group], stacked[...], NT)
        for inner in range(cols // piece):
            piece_out[group * (cols // piece) + inner] = part[inner * piece : (inner + 1) * piece].astype(piece_out.dtype)

    def piece_copy(slot_here, slot_there, peer):
        return pltpu.make_async_remote_copy(
            src_ref=piece_out.at[slot_here],
            dst_ref=piece_in.at[slot_there],
            send_sem=piece_send.at[slot_here],
            recv_sem=piece_recv.at[slot_there],
            device_id={"row": peer},
            device_id_type=MESH,
        )

    def sum_copy(slot_there, peer):
        return pltpu.make_async_remote_copy(
            src_ref=sum_out,
            dst_ref=sum_in.at[slot_there],
            send_sem=sum_send.at[peer],
            recv_sem=sum_recv.at[slot_there],
            device_id={"row": peer},
            device_id_type=MESH,
        )

    peers = [lax.rem(me + step, n_row) for step in range(1, n_row)]
    for peer in peers:
        piece_copy(peer, me, peer).start()
    piece_in[me] = piece_out[me]
    for peer in peers:
        piece_copy(peer, peer, peer).wait_recv()
    summed = piece_in[0].astype(jnp.float32)
    for peer in range(1, n_row):
        summed = summed + piece_in[peer].astype(jnp.float32)
    sum_out[...] = summed.astype(sum_out.dtype)
    for peer in peers:
        sum_copy(me, peer).start()
    sum_in[me] = sum_out[...]
    for peer in peers:
        sum_copy(peer, peer).wait_recv()
    for index in range(n_row):
        value = sum_in[index].astype(jnp.float32)
        gram[pl.ds(index * piece, piece), :] = value[:, :cols]
        projected[pl.ds(index * piece, piece), :] = value[:, cols:]

    for peer in peers:
        piece_copy(peer, me, peer).wait_send()
        sum_copy(me, peer).wait_send()
    for step in range(1, n_col):
        peer = lax.rem(mine + step, n_col)
        col_copy(mine, peer).wait_send()


def on_device(vectors, hblocks, counts, sources, send_rows):
    rows_here = hblocks.shape[0]
    cols, length = vectors.shape
    slots = send_rows.shape[0]
    n_row = lax.axis_size("row")
    n_col = lax.axis_size("col")
    assert slots == 2 * n_row
    live = lax.broadcasted_iota(jnp.int32, (rows_here, K), 1) < counts[:, None]
    hot = jax.nn.one_hot(jnp.where(live, sources, -1), rows_here + slots, dtype=jnp.bfloat16)
    u = jnp.einsum(
        "ikj,ikab->iajb", hot, hblocks.reshape(rows_here, K, B, B), preferred_element_type=jnp.float32
    ).astype(jnp.bfloat16).reshape(length, (rows_here + slots) * B)
    mask = jnp.repeat(jax.nn.one_hot(send_rows, rows_here, dtype=jnp.float32), B, axis=1)
    return run_filter(n_row, n_col, vectors, u, mask, send_rows)


def run_filter(n_row, n_col, vectors, u, mask, send_rows):
    cols, length = vectors.shape
    slots = send_rows.shape[0]
    total_cols = n_col * cols
    piece = total_cols // n_row
    sum_type = jnp.bfloat16 if piece % 16 == 0 else jnp.float32
    vmem = pl.BlockSpec(memory_space=pltpu.VMEM)
    dma = pltpu.SemaphoreType.DMA
    return pl.pallas_call(
        functools.partial(filter_kernel, n_row, n_col),
        out_shape=(
            jax.ShapeDtypeStruct((cols, length), jnp.bfloat16),
            jax.ShapeDtypeStruct((total_cols, cols), jnp.float32),
            jax.ShapeDtypeStruct((total_cols, cols), jnp.float32),
        ),
        in_specs=[pl.BlockSpec(memory_space=pltpu.SMEM), vmem, vmem, vmem],
        out_specs=(vmem, vmem, vmem),
        scratch_shapes=[
            pltpu.VMEM((cols, length), jnp.bfloat16),
            pltpu.VMEM((2 * cols, length), jnp.bfloat16),
            pltpu.VMEM((cols, length), jnp.float32),
            pltpu.VMEM((length // B, cols, PAIR), jnp.bfloat16),
            pltpu.VMEM((slots, cols, PAIR), jnp.float32),
            pltpu.VMEM((3, n_row, cols, 2 * PAIR), jnp.bfloat16),
            pltpu.VMEM((3, n_row, cols, 2 * PAIR), jnp.bfloat16),
            pltpu.VMEM((n_col, cols, length), jnp.bfloat16),
            pltpu.VMEM((n_row, piece, 2 * cols), sum_type),
            pltpu.VMEM((n_row, piece, 2 * cols), sum_type),
            pltpu.VMEM((piece, 2 * cols), sum_type),
            pltpu.VMEM((n_row, piece, 2 * cols), sum_type),
            dma((3, n_row)), dma((3, n_row)),
            dma((n_col,)), dma((n_col,)),
            dma((n_row,)), dma((n_row,)),
            dma((n_row,)), dma((n_row,)),
        ],
        compiler_params=pltpu.CompilerParams(
            collective_id=0, has_side_effects=True, vmem_limit_bytes=56 * 1024 * 1024
        ),
    )(send_rows, mask, vectors, u)


def solution(mesh):
    return jax.shard_map(
        on_device,
        mesh=mesh,
        in_specs=(P("col", "row"), P("row", None, None), P("row"), P("row", None), P("row")),
        out_specs=(P("col", "row"), P(None, "col"), P(None, "col")),
        check_vma=False,
    )
```

```python
import functools

import jax
import jax.numpy as jnp
from jax import lax
from jax.experimental import pallas as pl
from jax.experimental.pallas import tpu as pltpu
from jax.sharding import PartitionSpec as P

B = 64
K = 12
PAIR = 2 * B
TILE = 256
GROUP = 16
HALF = B // 2

center_value = 0.25
half_width = 1.5

MESH = pl.DeviceIdType.MESH
NN = (((1,), (0,)), ((), ()))
NT = (((1,), (1,)), ((), ()))


def dot(a, b, dims):
    return lax.dot_general(a, b, dims, preferred_element_type=jnp.float32)


def filter_kernel(
    n_row, n_col, chunk, index, key, x_in, h,
    filtered, gram, projected,
    ident, order, h_ordered, placed, upper, dense, diagonal, mask,
    x0, step_one, stacked, total, blocks, spread, upspread, out_buf, in_buf, gathered,
    piece_out, piece_in, sum_out, sum_in,
    send_sem, recv_sem, col_send, col_recv, piece_send, piece_recv, sum_send, sum_recv,
):
    me = lax.axis_index("row")
    mine = lax.axis_index("col")
    cols, length = x_in.shape
    rows = length // B
    pairs = length // PAIR
    slots = 2 * n_row
    named = rows + slots
    halves = named // 2
    tiles = length // TILE
    bf16 = jnp.bfloat16
    f32 = jnp.float32

    barrier = pltpu.get_barrier_semaphore()
    for step in range(1, n_row):
        pl.semaphore_signal(barrier, inc=1, device_id={"row": lax.rem(me + step, n_row)}, device_id_type=MESH)
    for step in range(1, n_col):
        pl.semaphore_signal(barrier, inc=1, device_id={"col": lax.rem(mine + step, n_col)}, device_id_type=MESH)

    def columns(at, width):
        return pl.ds(pl.multiple_of(at * width, width), width)

    def low_half(count):
        return lax.broadcasted_iota(jnp.int32, (count, PAIR), 1) < B

    low = low_half(cols)

    def both(values, where_low=low):
        turned = pltpu.roll(values, B, 1)
        return jnp.where(where_low, values, turned), jnp.where(where_low, turned, values)

    row_at = lax.broadcasted_iota(jnp.int32, (TILE, TILE), 0)
    col_at = lax.broadcasted_iota(jnp.int32, (TILE, TILE), 1)
    within = row_at & (B - 1)
    target = (row_at - within) + (within & 1) * HALF + (within >> 1)
    order[...] = jnp.where(target == col_at, 1.0, 0.0).astype(bf16)
    ident[...] = jnp.where(row_at == col_at, 1.0, 0.0).astype(bf16)

    lane_block = lax.broadcasted_iota(jnp.int32, (1, length), 1) >> 6

    def mask_body(slot, carry):
        mask[pl.ds(slot, 1), :] = jnp.where(lane_block == index[slot], 1.0, 0.0)
        return carry

    lax.fori_loop(0, slots, mask_body, 0)

    def keep_blocks(pair, values):
        first, second = both(values)
        blocks[2 * pair] = first.astype(bf16)
        blocks[2 * pair + 1] = second.astype(bf16)

    for tile in range(tiles):
        here = pl.ds(tile * TILE, TILE)
        value = dot(x_in[:, here], order[...], NN)
        x0[:, here] = value.astype(bf16)
        keep_blocks(2 * tile, value[:, :PAIR])
        keep_blocks(2 * tile + 1, value[:, PAIR:])

    def order_body(tile, carry):
        here = columns(tile, TILE)
        for group in range(rows // GROUP):
            part = h[:, pl.ds(group * GROUP, GROUP), here].reshape(K * GROUP, TILE)
            h_ordered[group, :, here] = dot(part, order[...], NN).astype(bf16)
        return carry

    lax.fori_loop(0, B * B // TILE, order_body, 0)

    count = chunk * named
    stride = count + 8
    per_group = GROUP // chunk
    low_rows = low_half(HALF)

    def chunk_body(at, carry):
        group = at // per_group
        inner = at % per_group
        names = lax.broadcasted_iota(jnp.int32, (count, K * GROUP), 0) + inner * count
        hot = jnp.where(names == key[group], 1.0, 0.0).astype(bf16)

        def place_body(tile, carry):
            value = dot(hot, h_ordered[group, :, columns(tile, TILE)], NN)
            placed[pl.ds(pl.multiple_of(2 * tile * stride, 8), count), :] = value[:, :PAIR]
            placed[pl.ds(pl.multiple_of((2 * tile + 1) * stride, 8), count), :] = value[:, PAIR:]
            return carry

        lax.fori_loop(0, B * B // TILE, place_body, 0)

        def turn_body(row, carry):
            for pair in range(halves):
                base = row * named + pair
                first = placed[pl.ds(base, HALF, stride=stride), :]
                second = placed[pl.ds(base + halves, HALF, stride=stride), :]
                even = jnp.where(low_rows, first, pltpu.roll(second, B, 1))
                odd = jnp.where(low_rows, pltpu.roll(first, B, 1), second)
                here = pl.ds(pair * PAIR, PAIR)
                upper[at * chunk + row, pl.ds(0, HALF), here] = even.astype(bf16)
                upper[at * chunk + row, pl.ds(HALF, HALF), here] = odd.astype(bf16)
            return carry

        lax.fori_loop(0, chunk, turn_body, 0)
        return carry

    lax.fori_loop(0, rows // chunk, chunk_body, 0)

    low_block = low_half(B)
    diagonal[...] = jnp.zeros_like(diagonal)
    for slot in range(slots):
        here = pl.ds(length + (slot // 2) * PAIR, PAIR)
        value = upper[index[slots + slot], :, here].astype(f32)
        keep = low_block if slot % 2 == 0 else jnp.logical_not(low_block)
        part = slot % 4
        diagonal[slot // 4, pl.ds(part * B, B), pl.ds((part // 2) * PAIR, PAIR)] = jnp.where(keep, value, 0.0).astype(bf16)

    per_tile = TILE // B

    def dense_body(tile, carry):
        for other in range(tiles):
            there = upper[pl.ds(other * per_tile, per_tile), :, columns(tile, TILE)].reshape(TILE, TILE)
            straight = upper[pl.ds(tile * per_tile, per_tile), :, pl.ds(other * TILE, TILE)].reshape(TILE, TILE)
            value = dot(ident[...], there, NT) + straight.astype(f32)
            dense[columns(tile, TILE), pl.ds(other * TILE, TILE)] = value.astype(bf16)
        return carry

    lax.fori_loop(0, tiles, dense_body, 0)
    upspread[slots] = jnp.zeros((cols, PAIR), f32)

    pl.semaphore_wait(barrier, n_row + n_col - 2)

    def row_copy(phase, slot_here, slot_there, peer):
        return pltpu.make_async_remote_copy(
            src_ref=out_buf.at[phase, slot_here],
            dst_ref=in_buf.at[phase, slot_there],
            send_sem=send_sem.at[phase, slot_here],
            recv_sem=recv_sem.at[phase, slot_there],
            device_id={"row": peer},
            device_id_type=MESH,
        )

    def pick(first, second):
        return jnp.where(low, blocks[first].astype(f32), blocks[second].astype(f32)).astype(bf16)

    def apply_operator(phase, source, finish, beside):
        for pack in range(slots // 4):
            at = slots + 4 * pack
            near = jnp.concatenate([pick(index[at], index[at + 1]), pick(index[at + 2], index[at + 3])], 1)
            product = dot(near, diagonal[pack], NN).astype(bf16)
            for inner in range(2):
                peer = 2 * pack + inner
                out_buf[phase, peer, :, pl.ds(0, PAIR)] = pick(index[2 * peer], index[2 * peer + 1])
                out_buf[phase, peer, :, pl.ds(PAIR, PAIR)] = product[:, inner * PAIR : (inner + 1) * PAIR]
        for step in range(1, n_row):
            peer = lax.rem(me + step, n_row)
            row_copy(phase, peer, me, peer).start()
        in_buf[phase, me] = out_buf[phase, me]

        def local_body(tile, carry):
            here = columns(tile, TILE)
            total[:, here] = dot(source[...], dense[:, here], NN)
            return carry

        lax.fori_loop(0, tiles, local_body, 0)
        beside()
        for step in range(1, n_row):
            peer = lax.rem(me + step, n_row)
            row_copy(phase, peer, peer, peer).wait_recv()

        for pack in range(slots // 4):
            far = jnp.concatenate([in_buf[phase, 2 * pack + inner, :, pl.ds(0, PAIR)] for inner in range(2)], 1)
            product = dot(far, diagonal[pack], NT)
            for inner in range(2):
                peer = 2 * pack + inner
                first, second = both(product[:, inner * PAIR : (inner + 1) * PAIR])
                upspread[2 * peer] = first
                upspread[2 * peer + 1] = second
                first, second = both(in_buf[phase, peer, :, pl.ds(PAIR, PAIR)].astype(f32))
                spread[2 * peer] = first
                spread[2 * peer + 1] = second

        def finish_body(pair, carry):
            here = columns(pair, PAIR)
            at = 2 * slots + 4 * pair
            value = total[:, here] + jnp.where(
                low,
                upspread[index[at]] + upspread[index[at + 1]],
                upspread[index[at + 2]] + upspread[index[at + 3]],
            )
            for slot in range(slots):
                value = value + spread[slot] * mask[pl.ds(slot, 1), here]
            finish(pair, here, value)
            return carry

        lax.fori_loop(0, pairs, finish_body, 0)

    def first_finish(pair, here, value):
        new = ((value - center_value * x0[:, here].astype(f32)) / half_width).astype(bf16)
        step_one[:, here] = new
        keep_blocks(pair, new.astype(f32))

    def second_finish(pair, here, value):
        old = step_one[:, here].astype(f32)
        new = (2.0 * (value - center_value * old) / half_width - x0[:, here].astype(f32)).astype(bf16)
        stacked[pl.ds(0, cols), here] = new
        gathered[mine, :, here] = new
        keep_blocks(pair, new.astype(f32))

    def third_finish(pair, here, value):
        stacked[pl.ds(cols, cols), here] = value.astype(bf16)

    def nothing():
        pass

    def write_filtered():
        for tile in range(tiles):
            here = pl.ds(tile * TILE, TILE)
            filtered[:, here] = dot(stacked[pl.ds(0, cols), here], order[...], NT).astype(bf16)

    def col_copy(slot, peer):
        return pltpu.make_async_remote_copy(
            src_ref=gathered.at[mine],
            dst_ref=gathered.at[slot],
            send_sem=col_send.at[peer],
            recv_sem=col_recv.at[slot],
            device_id={"col": peer},
            device_id_type=MESH,
        )

    apply_operator(0, x0, first_finish, nothing)
    apply_operator(1, step_one, second_finish, nothing)
    for step in range(1, n_col):
        peer = lax.rem(mine + step, n_col)
        col_copy(mine, peer).start()
    apply_operator(2, stacked.at[pl.ds(0, cols)], third_finish, write_filtered)
    for step in range(1, n_col):
        peer = lax.rem(mine + step, n_col)
        col_copy(peer, peer).wait_recv()

    piece = 2 * cols // n_row
    part = dot(stacked[...], gathered[...].reshape(n_col * cols, length), NT)
    for at in range(n_row):
        piece_out[at] = part[at * piece : (at + 1) * piece].astype(piece_out.dtype)

    def piece_copy(slot_here, slot_there, peer):
        return pltpu.make_async_remote_copy(
            src_ref=piece_out.at[slot_here],
            dst_ref=piece_in.at[slot_there],
            send_sem=piece_send.at[slot_here],
            recv_sem=piece_recv.at[slot_there],
            device_id={"row": peer},
            device_id_type=MESH,
        )

    def sum_copy(slot_there, peer):
        return pltpu.make_async_remote_copy(
            src_ref=sum_out,
            dst_ref=sum_in.at[slot_there],
            send_sem=sum_send.at[peer],
            recv_sem=sum_recv.at[slot_there],
            device_id={"row": peer},
            device_id_type=MESH,
        )

    peers = [lax.rem(me + step, n_row) for step in range(1, n_row)]
    for peer in peers:
        piece_copy(peer, me, peer).start()
    piece_in[me] = piece_out[me]
    for peer in peers:
        piece_copy(peer, peer, peer).wait_recv()
    summed = piece_in[0].astype(f32)
    for peer in range(1, n_row):
        summed = summed + piece_in[peer].astype(f32)
    sum_out[...] = summed.astype(sum_out.dtype)
    for peer in peers:
        sum_copy(me, peer).start()
    sum_in[me] = sum_out[...]
    for peer in peers:
        sum_copy(peer, peer).wait_recv()
    for at in range(n_row):
        value = sum_in[at].astype(f32)
        first = at * piece
        if first < cols:
            gram[pl.ds(first, piece), :] = value
        else:
            projected[pl.ds(first - cols, piece), :] = value

    for peer in peers:
        for phase in range(3):
            row_copy(phase, peer, me, peer).wait_send()
        piece_copy(peer, me, peer).wait_send()
        sum_copy(me, peer).wait_send()
    for step in range(1, n_col):
        peer = lax.rem(mine + step, n_col)
        col_copy(mine, peer).wait_send()


def on_device(vectors, hblocks, counts, sources, send_rows):
    rows = hblocks.shape[0]
    cols, length = vectors.shape
    slots = send_rows.shape[0]
    n_row = lax.axis_size("row")
    n_col = lax.axis_size("col")
    assert slots == 2 * n_row
    named = rows + slots
    live = lax.broadcasted_iota(jnp.int32, (rows, K), 1) < counts[:, None]
    place = (jnp.arange(rows, dtype=jnp.int32) % GROUP)[:, None] * named
    key = jnp.where(live, place + (sources % 2) * (named // 2) + sources // 2, -1)
    key = key.reshape(rows // GROUP, GROUP, K).transpose(0, 2, 1).reshape(rows // GROUP, 1, K * GROUP)
    near = sources[:, 1:3]
    which = near[:, :, None] == rows + jnp.arange(slots, dtype=jnp.int32)
    holder = jnp.sum(jnp.where(which, jnp.arange(rows, dtype=jnp.int32)[:, None, None], 0), (0, 1), dtype=jnp.int32)
    entry = jnp.where(near >= rows, near - rows, slots).reshape(-1)
    index = jnp.concatenate([send_rows, holder, entry])

    total_cols = n_col * cols
    piece = 2 * cols // n_row
    sum_type = jnp.bfloat16 if piece % 16 == 0 else jnp.float32
    chunk = 8 if named <= 48 else 4
    vmem = pl.BlockSpec(memory_space=pltpu.VMEM)
    dma = pltpu.SemaphoreType.DMA
    bf16 = jnp.bfloat16
    f32 = jnp.float32
    filtered, gram, projected = pl.pallas_call(
        functools.partial(filter_kernel, n_row, n_col, chunk),
        out_shape=(
            jax.ShapeDtypeStruct((cols, length), bf16),
            jax.ShapeDtypeStruct((cols, total_cols), f32),
            jax.ShapeDtypeStruct((cols, total_cols), f32),
        ),
        in_specs=[pl.BlockSpec(memory_space=pltpu.SMEM), vmem, vmem, vmem],
        out_specs=(vmem, vmem, vmem),
        scratch_shapes=[
            pltpu.VMEM((TILE, TILE), bf16),
            pltpu.VMEM((TILE, TILE), bf16),
            pltpu.VMEM((rows // GROUP, K * GROUP, B * B), bf16),
            pltpu.VMEM((HALF * (chunk * named + 8), PAIR), f32),
            pltpu.VMEM((rows, B, named * B), bf16),
            pltpu.VMEM((length, length), bf16),
            pltpu.VMEM((slots // 4, TILE, TILE), bf16),
            pltpu.VMEM((slots, length), f32),
            pltpu.VMEM((cols, length), bf16),
            pltpu.VMEM((cols, length), bf16),
            pltpu.VMEM((2 * cols, length), bf16),
            pltpu.VMEM((cols, length), f32),
            pltpu.VMEM((rows, cols, PAIR), bf16),
            pltpu.VMEM((slots, cols, PAIR), f32),
            pltpu.VMEM((slots + 1, cols, PAIR), f32),
            pltpu.VMEM((3, n_row, cols, 2 * PAIR), bf16),
            pltpu.VMEM((3, n_row, cols, 2 * PAIR), bf16),
            pltpu.VMEM((n_col, cols, length), bf16),
            pltpu.VMEM((n_row, piece, total_cols), sum_type),
            pltpu.VMEM((n_row, piece, total_cols), sum_type),
            pltpu.VMEM((piece, total_cols), sum_type),
            pltpu.VMEM((n_row, piece, total_cols), sum_type),
            dma((3, n_row)), dma((3, n_row)),
            dma((n_col,)), dma((n_col,)),
            dma((n_row,)), dma((n_row,)),
            dma((n_row,)), dma((n_row,)),
        ],
        compiler_params=pltpu.CompilerParams(
            collective_id=0, has_side_effects=True, vmem_limit_bytes=60 * 1024 * 1024
        ),
    )(index, key, vectors, hblocks.transpose(1, 0, 2))
    return filtered, gram.T, projected.T


def solution(mesh):
    return jax.shard_map(
        on_device,
        mesh=mesh,
        in_specs=(P("col", "row"), P("row", None, None), P("row"), P("row", None), P("row")),
        out_specs=(P("col", "row"), P(None, "col"), P(None, "col")),
        check_vma=False,
    )
```

```python
import functools

import jax
import jax.numpy as jnp
from jax import lax
from jax.experimental import pallas as pl
from jax.experimental.pallas import tpu as pltpu
from jax.sharding import PartitionSpec as P

B = 64
K = 12
PAIR = 2 * B
TILE = 256
UNROLL = 4
HALF = B // 2

center_value = 0.25
half_width = 1.5

MESH = pl.DeviceIdType.MESH
NN = (((1,), (0,)), ((), ()))
NT = (((1,), (1,)), ((), ()))


def dot(a, b, dims):
    return lax.dot_general(a, b, dims, preferred_element_type=jnp.float32)


def order_matrix():
    row_at = lax.broadcasted_iota(jnp.int32, (TILE, TILE), 0)
    col_at = lax.broadcasted_iota(jnp.int32, (TILE, TILE), 1)
    within = row_at & (B - 1)
    target = (row_at - within) + (within & 1) * HALF + (within >> 1)
    return jnp.where(target == col_at, 1.0, 0.0).astype(jnp.bfloat16)


def build_kernel(rows, slots, sources, counts, h, dense, diagonal, holder, order, ident, placed, upper):
    step = pl.program_id(0)
    per_tile = TILE // B
    tiles = rows // per_tile
    stride = rows + 8
    bf16 = jnp.bfloat16

    @pl.when(step == 0)
    def _():
        order[...] = order_matrix()
        row_at = lax.broadcasted_iota(jnp.int32, (TILE, TILE), 0)
        col_at = lax.broadcasted_iota(jnp.int32, (TILE, TILE), 1)
        ident[...] = jnp.where(row_at == col_at, 1.0, 0.0).astype(bf16)
        diagonal[...] = jnp.zeros_like(diagonal)

        def clear_body(row, carry):
            upper[row] = jnp.zeros_like(upper[row])
            return carry

        lax.fori_loop(0, rows, clear_body, 0)

        def holder_body(row, carry):
            for slot in (1, 2):
                source = sources[slot, row]

                @pl.when(source >= rows)
                def _():
                    holder[source - rows] = row

            return carry

        lax.fori_loop(0, rows, holder_body, 0)

    @pl.when(step < K)
    def _():
        pieces = B * B // TILE
        lanes = jnp.concatenate([h[0, :, at * TILE : (at + 1) * TILE] for at in range(pieces)], 0)
        value = dot(lanes, order[...], NN)
        for at in range(pieces):
            part = value[at * rows : (at + 1) * rows]
            placed[pl.ds(2 * at * stride, rows), :] = part[:, :PAIR]
            placed[pl.ds((2 * at + 1) * stride, rows), :] = part[:, PAIR:]
        side = lax.broadcasted_iota(jnp.int32, (HALF, PAIR), 1) >> 6

        def add_body(group, carry):
            news = []
            for inner in range(UNROLL):
                row = group * UNROLL + inner
                source = sources[step, row]
                half = source & 1
                wanted = jnp.where(step < counts[row], half, 2)
                straight = placed[pl.ds(row, HALF, stride=stride), :]
                turned = pltpu.roll(straight, B, 1)
                keep = side == wanted
                first = jnp.broadcast_to(half, (HALF, PAIR)) == 0
                even = jnp.where(keep, jnp.where(first, straight, turned), 0.0)
                odd = jnp.where(keep, jnp.where(first, turned, straight), 0.0)
                old = upper[row, source >> 1]
                news.append((row, source >> 1, old + jnp.concatenate([even, odd], 0).astype(bf16)))
            for row, pair, new in news:
                upper[row, pair] = new
            return carry

        lax.fori_loop(0, rows // UNROLL, add_body, 0)

    @pl.when(step >= K)
    def _():
        tile = step - K
        for other in range(tiles):
            def block(at_row, at_col):
                return jnp.concatenate(
                    [
                        upper[pl.ds(at_row * per_tile, per_tile), 2 * at_col + side].reshape(TILE, PAIR)
                        for side in range(2)
                    ],
                    1,
                )

            value = dot(ident[...], block(tile, other), NT) + block(other, tile).astype(jnp.float32)
            dense[0, pl.ds(other * TILE, TILE), :] = value.astype(bf16)

    @pl.when(step == K + tiles - 1)
    def _():
        low = lax.broadcasted_iota(jnp.int32, (B, PAIR), 1) < B
        for slot in range(slots):
            value = upper[holder[slot], (rows + slot) // 2].astype(jnp.float32)
            keep = low if slot % 2 == 0 else jnp.logical_not(low)
            part = slot % 4
            diagonal[slot // 4, pl.ds(part * B, B), pl.ds((part // 2) * PAIR, PAIR)] = jnp.where(
                keep, value, 0.0
            ).astype(bf16)


def output_kernel(cols, ordered, sums, filtered, gram, projected):
    order = order_matrix()
    for tile in range(ordered.shape[1] // TILE):
        here = pl.ds(tile * TILE, TILE)
        filtered[:, here] = dot(ordered[:, here], order, NT).astype(jnp.bfloat16)
    count, piece = sums.shape[0], sums.shape[1]
    for at in range(count):
        value = sums[at].astype(jnp.float32)
        first = at * piece
        if first < cols:
            gram[pl.ds(first, piece), :] = value
        else:
            projected[pl.ds(first - cols, piece), :] = value


def filter_kernel(
    n_row, n_col, send_rows, sources, holder, x_in, diagonal, dense_in,
    filtered, sum_in,
    dense, mask,
    x0, step_one, stacked, total, blocks, spread, upspread, out_buf, in_buf, gathered,
    piece_out, piece_in, sum_out,
    dense_sem,
    send_sem, recv_sem, col_send, col_recv, piece_send, piece_recv, sum_send, sum_recv,
):
    me = lax.axis_index("row")
    mine = lax.axis_index("col")
    cols, length = x_in.shape
    rows = length // B
    pairs = length // PAIR
    slots = 2 * n_row
    tiles = length // TILE
    bf16 = jnp.bfloat16
    f32 = jnp.float32

    barrier = pltpu.get_barrier_semaphore()
    for step in range(1, n_row):
        pl.semaphore_signal(barrier, inc=1, device_id={"row": lax.rem(me + step, n_row)}, device_id_type=MESH)
    for step in range(1, n_col):
        pl.semaphore_signal(barrier, inc=1, device_id={"col": lax.rem(mine + step, n_col)}, device_id_type=MESH)

    def dense_copy(tile):
        return pltpu.make_async_copy(dense_in.at[tile], dense.at[tile], dense_sem.at[tile])

    for tile in range(tiles):
        dense_copy(tile).start()

    def columns(at, width):
        return pl.ds(pl.multiple_of(at * width, width), width)

    low = lax.broadcasted_iota(jnp.int32, (cols, PAIR), 1) < B

    def both(values):
        turned = pltpu.roll(values, B, 1)
        return jnp.where(low, values, turned), jnp.where(low, turned, values)

    lane_block = lax.broadcasted_iota(jnp.int32, (1, length), 1) >> 6

    def mask_body(slot, carry):
        mask[pl.ds(slot, 1), :] = jnp.where(lane_block == send_rows[slot], 1.0, 0.0)
        return carry

    lax.fori_loop(0, slots, mask_body, 0)

    def keep_blocks(pair, values):
        first, second = both(values)
        blocks[2 * pair] = first.astype(bf16)
        blocks[2 * pair + 1] = second.astype(bf16)

    order = order_matrix()
    for tile in range(tiles):
        here = pl.ds(tile * TILE, TILE)
        value = dot(x_in[:, here], order, NN)
        x0[:, here] = value.astype(bf16)
        keep_blocks(2 * tile, value[:, :PAIR])
        keep_blocks(2 * tile + 1, value[:, PAIR:])

    upspread[slots] = jnp.zeros((cols, PAIR), f32)

    def arrived_at(row, slot):
        source = sources[slot, row]
        return upspread[jnp.where(source >= rows, source - rows, slots)]

    pl.semaphore_wait(barrier, n_row + n_col - 2)

    def row_copy(phase, slot_here, slot_there, peer):
        return pltpu.make_async_remote_copy(
            src_ref=out_buf.at[phase, slot_here],
            dst_ref=in_buf.at[phase, slot_there],
            send_sem=send_sem.at[phase, slot_here],
            recv_sem=recv_sem.at[phase, slot_there],
            device_id={"row": peer},
            device_id_type=MESH,
        )

    def pick(first, second):
        return jnp.where(low, blocks[first].astype(f32), blocks[second].astype(f32)).astype(bf16)

    def apply_operator(phase, source, finish):
        for pack in range(slots // 4):
            at = 4 * pack
            near = jnp.concatenate([pick(holder[at], holder[at + 1]), pick(holder[at + 2], holder[at + 3])], 1)
            product = dot(near, diagonal[pack], NN).astype(bf16)
            for inner in range(2):
                peer = 2 * pack + inner
                out_buf[phase, peer, :, pl.ds(0, PAIR)] = pick(send_rows[2 * peer], send_rows[2 * peer + 1])
                out_buf[phase, peer, :, pl.ds(PAIR, PAIR)] = product[:, inner * PAIR : (inner + 1) * PAIR]
        for step in range(1, n_row):
            peer = lax.rem(me + step, n_row)
            row_copy(phase, peer, me, peer).start()
        in_buf[phase, me] = out_buf[phase, me]

        def local_body(tile, carry):
            if phase == 0:
                dense_copy(tile).wait()
            total[:, columns(tile, TILE)] = dot(source[...], dense[tile], NN)
            return carry

        lax.fori_loop(0, tiles, local_body, 0)
        for step in range(1, n_row):
            peer = lax.rem(me + step, n_row)
            row_copy(phase, peer, peer, peer).wait_recv()

        for pack in range(slots // 4):
            far = jnp.concatenate([in_buf[phase, 2 * pack + inner, :, pl.ds(0, PAIR)] for inner in range(2)], 1)
            product = dot(far, diagonal[pack], NT)
            for inner in range(2):
                peer = 2 * pack + inner
                first, second = both(product[:, inner * PAIR : (inner + 1) * PAIR])
                upspread[2 * peer] = first
                upspread[2 * peer + 1] = second
                first, second = both(in_buf[phase, peer, :, pl.ds(PAIR, PAIR)].astype(f32))
                spread[2 * peer] = first
                spread[2 * peer + 1] = second

        def finish_body(pair, carry):
            here = columns(pair, PAIR)
            value = total[:, here] + jnp.where(
                low,
                arrived_at(2 * pair, 1) + arrived_at(2 * pair, 2),
                arrived_at(2 * pair + 1, 1) + arrived_at(2 * pair + 1, 2),
            )
            for slot in range(slots):
                value = value + spread[slot] * mask[pl.ds(slot, 1), here]
            finish(pair, here, value)
            return carry

        lax.fori_loop(0, pairs, finish_body, 0)

    def first_finish(pair, here, value):
        new = ((value - center_value * x0[:, here].astype(f32)) / half_width).astype(bf16)
        step_one[:, here] = new
        keep_blocks(pair, new.astype(f32))

    def second_finish(pair, here, value):
        old = step_one[:, here].astype(f32)
        new = (2.0 * (value - center_value * old) / half_width - x0[:, here].astype(f32)).astype(bf16)
        stacked[pl.ds(0, cols), here] = new
        gathered[mine, :, here] = new
        filtered[:, here] = new
        keep_blocks(pair, new.astype(f32))

    def third_finish(pair, here, value):
        stacked[pl.ds(cols, cols), here] = value.astype(bf16)

    def col_copy(slot, peer):
        return pltpu.make_async_remote_copy(
            src_ref=gathered.at[mine],
            dst_ref=gathered.at[slot],
            send_sem=col_send.at[peer],
            recv_sem=col_recv.at[slot],
            device_id={"col": peer},
            device_id_type=MESH,
        )

    apply_operator(0, x0, first_finish)
    apply_operator(1, step_one, second_finish)
    for step in range(1, n_col):
        peer = lax.rem(mine + step, n_col)
        col_copy(mine, peer).start()
    apply_operator(2, stacked.at[pl.ds(0, cols)], third_finish)
    for step in range(1, n_col):
        peer = lax.rem(mine + step, n_col)
        col_copy(peer, peer).wait_recv()

    piece = 2 * cols // n_row
    part = dot(stacked[...], gathered[...].reshape(n_col * cols, length), NT)
    for at in range(n_row):
        piece_out[at] = part[at * piece : (at + 1) * piece].astype(piece_out.dtype)

    def piece_copy(slot_here, slot_there, peer):
        return pltpu.make_async_remote_copy(
            src_ref=piece_out.at[slot_here],
            dst_ref=piece_in.at[slot_there],
            send_sem=piece_send.at[slot_here],
            recv_sem=piece_recv.at[slot_there],
            device_id={"row": peer},
            device_id_type=MESH,
        )

    def sum_copy(slot_there, peer):
        return pltpu.make_async_remote_copy(
            src_ref=sum_out,
            dst_ref=sum_in.at[slot_there],
            send_sem=sum_send.at[peer],
            recv_sem=sum_recv.at[slot_there],
            device_id={"row": peer},
            device_id_type=MESH,
        )

    peers = [lax.rem(me + step, n_row) for step in range(1, n_row)]
    for peer in peers:
        piece_copy(peer, me, peer).start()
    piece_in[me] = piece_out[me]
    for peer in peers:
        piece_copy(peer, peer, peer).wait_recv()
    summed = piece_in[0].astype(f32)
    for peer in range(1, n_row):
        summed = summed + piece_in[peer].astype(f32)
    sum_out[...] = summed.astype(sum_out.dtype)
    for peer in peers:
        sum_copy(me, peer).start()
    sum_in[me] = sum_out[...]
    for peer in peers:
        sum_copy(peer, peer).wait_recv()
    for peer in peers:
        for phase in range(3):
            row_copy(phase, peer, me, peer).wait_send()
        piece_copy(peer, me, peer).wait_send()
        sum_copy(me, peer).wait_send()
    for step in range(1, n_col):
        peer = lax.rem(mine + step, n_col)
        col_copy(mine, peer).wait_send()


def on_device(vectors, hblocks, counts, sources, send_rows):
    rows = hblocks.shape[0]
    cols, length = vectors.shape
    slots = send_rows.shape[0]
    n_row = lax.axis_size("row")
    n_col = lax.axis_size("col")
    assert slots == 2 * n_row
    named = rows + slots
    tiles = length // TILE
    total_cols = n_col * cols
    piece = 2 * cols // n_row
    sum_type = jnp.bfloat16 if piece % 16 == 0 else jnp.float32
    smem = pl.BlockSpec(memory_space=pltpu.SMEM)
    vmem = pl.BlockSpec(memory_space=pltpu.VMEM)
    dma = pltpu.SemaphoreType.DMA
    bf16 = jnp.bfloat16
    f32 = jnp.float32
    by_slot = sources.T
    dense, diagonal, holder = pl.pallas_call(
        functools.partial(build_kernel, rows, slots),
        grid=(K + tiles,),
        out_shape=(
            jax.ShapeDtypeStruct((tiles, length, TILE), bf16),
            jax.ShapeDtypeStruct((slots // 4, TILE, TILE), bf16),
            jax.ShapeDtypeStruct((slots,), jnp.int32),
        ),
        in_specs=[smem, smem, pl.BlockSpec((1, rows, B * B), lambda step: (jnp.minimum(step, K - 1), 0, 0))],
        out_specs=(
            pl.BlockSpec((1, length, TILE), lambda step: (jnp.maximum(step - K, 0), 0, 0)),
            pl.BlockSpec((slots // 4, TILE, TILE), lambda step: (0, 0, 0)),
            smem,
        ),
        scratch_shapes=[
            pltpu.VMEM((TILE, TILE), bf16),
            pltpu.VMEM((TILE, TILE), bf16),
            pltpu.VMEM((HALF * (rows + 8), PAIR), f32),
            pltpu.VMEM((rows, named // 2, B, PAIR), bf16),
        ],
        compiler_params=pltpu.CompilerParams(vmem_limit_bytes=56 * 1024 * 1024),
    )(by_slot, counts, hblocks.transpose(1, 0, 2))

    ordered, sums = pl.pallas_call(
        functools.partial(filter_kernel, n_row, n_col),
        out_shape=(
            jax.ShapeDtypeStruct((cols, length), bf16),
            jax.ShapeDtypeStruct((n_row, piece, total_cols), sum_type),
        ),
        in_specs=[smem, smem, smem, vmem, vmem, pl.BlockSpec(memory_space=pl.ANY)],
        out_specs=(vmem, vmem),
        scratch_shapes=[
            pltpu.VMEM((tiles, length, TILE), bf16),
            pltpu.VMEM((slots, length), f32),
            pltpu.VMEM((cols, length), bf16),
            pltpu.VMEM((cols, length), bf16),
            pltpu.VMEM((2 * cols, length), bf16),
            pltpu.VMEM((cols, length), f32),
            pltpu.VMEM((rows, cols, PAIR), bf16),
            pltpu.VMEM((slots, cols, PAIR), f32),
            pltpu.VMEM((slots + 1, cols, PAIR), f32),
            pltpu.VMEM((3, n_row, cols, 2 * PAIR), bf16),
            pltpu.VMEM((3, n_row, cols, 2 * PAIR), bf16),
            pltpu.VMEM((n_col, cols, length), bf16),
            pltpu.VMEM((n_row, piece, total_cols), sum_type),
            pltpu.VMEM((n_row, piece, total_cols), sum_type),
            pltpu.VMEM((piece, total_cols), sum_type),
            dma((tiles,)),
            dma((3, n_row)), dma((3, n_row)),
            dma((n_col,)), dma((n_col,)),
            dma((n_row,)), dma((n_row,)),
            dma((n_row,)), dma((n_row,)),
        ],
        compiler_params=pltpu.CompilerParams(
            collective_id=0, has_side_effects=True, vmem_limit_bytes=56 * 1024 * 1024
        ),
    )(send_rows, by_slot, holder, vectors, diagonal, dense)

    filtered, gram, projected = pl.pallas_call(
        functools.partial(output_kernel, cols),
        out_shape=(
            jax.ShapeDtypeStruct((cols, length), bf16),
            jax.ShapeDtypeStruct((cols, total_cols), f32),
            jax.ShapeDtypeStruct((cols, total_cols), f32),
        ),
        in_specs=[vmem, vmem],
        out_specs=(vmem, vmem, vmem),
    )(ordered, sums)
    return filtered, gram.T, projected.T


def solution(mesh):
    return jax.shard_map(
        on_device,
        mesh=mesh,
        in_specs=(P("col", "row"), P("row", None, None), P("row"), P("row", None), P("row")),
        out_specs=(P("col", "row"), P(None, "col"), P(None, "col")),
        check_vma=False,
    )
```

```python
import functools

import jax
import jax.numpy as jnp
from jax import lax
from jax.experimental import pallas as pl
from jax.experimental.pallas import tpu as pltpu
from jax.sharding import PartitionSpec as P

B = 64
K = 12
PAIR = 2 * B
TILE = 256
UNROLL = 8
SLOTS_STEP = 3
TILES_STEP = 2
HALF = B // 2

center_value = 0.25
half_width = 1.5

MESH = pl.DeviceIdType.MESH
NN = (((1,), (0,)), ((), ()))
NT = (((1,), (1,)), ((), ()))


def dot(a, b, dims):
    return lax.dot_general(a, b, dims, preferred_element_type=jnp.float32)


def order_matrix(turned=0):
    row_at = lax.broadcasted_iota(jnp.int32, (TILE, TILE), 0)
    col_at = lax.broadcasted_iota(jnp.int32, (TILE, TILE), 1)
    within = row_at & (B - 1)
    target = (row_at - within) + (within & 1) * HALF + (within >> 1)
    target = target ^ turned
    return jnp.where(target == col_at, 1.0, 0.0).astype(jnp.bfloat16)


def build_kernel(rows, slots, sources, counts, h, dense, diagonal, holder, order, order_turned, ident, placed, upper):
    step = pl.program_id(0)
    per_tile = TILE // B
    tiles = rows // per_tile
    stride = rows + 8
    size = HALF * stride
    place_steps = K // SLOTS_STEP
    bf16 = jnp.bfloat16

    @pl.when(step == 0)
    def _():
        order[...] = order_matrix()
        order_turned[...] = order_matrix(B)
        row_at = lax.broadcasted_iota(jnp.int32, (TILE, TILE), 0)
        col_at = lax.broadcasted_iota(jnp.int32, (TILE, TILE), 1)
        ident[...] = jnp.where(row_at == col_at, 1.0, 0.0).astype(bf16)
        diagonal[...] = jnp.zeros_like(diagonal)

        def clear_body(row, carry):
            upper[row] = jnp.zeros_like(upper[row])
            return carry

        lax.fori_loop(0, rows, clear_body, 0)

        def holder_body(row, carry):
            for slot in (1, 2):
                source = sources[slot, row]

                @pl.when(source >= rows)
                def _():
                    holder[source - rows] = row

            return carry

        lax.fori_loop(0, rows, holder_body, 0)

    @pl.when(step < place_steps)
    def _():
        pieces = B * B // TILE
        side = lax.broadcasted_iota(jnp.int32, (HALF, PAIR), 1) >> 6

        def slot_body(inner_slot, carry):
            slot = step * SLOTS_STEP + inner_slot
            lanes = jnp.concatenate([h[inner_slot, :, at * TILE : (at + 1) * TILE] for at in range(pieces)], 0)
            for turned, matrix in enumerate((order, order_turned)):
                value = dot(lanes, matrix[...], NN)
                for at in range(pieces):
                    part = value[at * rows : (at + 1) * rows]
                    placed[pl.ds(turned * size + 2 * at * stride, rows), :] = part[:, :PAIR]
                    placed[pl.ds(turned * size + (2 * at + 1) * stride, rows), :] = part[:, PAIR:]

            def add_body(group, carry):
                news = []
                for inner in range(UNROLL):
                    row = group * UNROLL + inner
                    source = sources[slot, row]
                    half = source & 1
                    keep = side == jnp.where(slot < counts[row], half, 2)
                    even = placed[pl.ds(half * size + row, HALF, stride=stride), :]
                    odd = placed[pl.ds((1 - half) * size + row, HALF, stride=stride), :]
                    even = jnp.where(keep, even, 0.0).astype(bf16)
                    odd = jnp.where(keep, odd, 0.0).astype(bf16)
                    old = upper[row, source >> 1]
                    news.append((row, source >> 1, old + jnp.concatenate([even, odd], 0)))
                for row, pair, new in news:
                    upper[row, pair] = new
                return carry

            return lax.fori_loop(0, rows // UNROLL, add_body, carry)

        lax.fori_loop(0, SLOTS_STEP, slot_body, 0)

    @pl.when(step >= place_steps)
    def _():
        for inner, other in [(inner, other) for inner in range(TILES_STEP) for other in range(tiles)]:
            tile = (step - place_steps) * TILES_STEP + inner

            def block(at_row, at_col):
                return jnp.concatenate(
                    [
                        upper[pl.ds(at_row * per_tile, per_tile), 2 * at_col + side].reshape(TILE, PAIR)
                        for side in range(2)
                    ],
                    1,
                )

            value = dot(ident[...], block(tile, other), NT) + block(other, tile).astype(jnp.float32)
            dense[inner, pl.ds(other * TILE, TILE), :] = value.astype(bf16)

    @pl.when(step == pl.num_programs(0) - 1)
    def _():
        low = lax.broadcasted_iota(jnp.int32, (B, PAIR), 1) < B
        for slot in range(slots):
            value = upper[holder[slot], (rows + slot) // 2].astype(jnp.float32)
            keep = low if slot % 2 == 0 else jnp.logical_not(low)
            part = slot % 4
            diagonal[slot // 4, pl.ds(part * B, B), pl.ds((part // 2) * PAIR, PAIR)] = jnp.where(
                keep, value, 0.0
            ).astype(bf16)


def output_kernel(cols, ordered, sums, filtered, gram, projected):
    order = order_matrix()
    for tile in range(ordered.shape[1] // TILE):
        here = pl.ds(tile * TILE, TILE)
        filtered[:, here] = dot(ordered[:, here], order, NT).astype(jnp.bfloat16)
    count, piece = sums.shape[0], sums.shape[1]
    for at in range(count):
        value = sums[at].astype(jnp.float32)
        first = at * piece
        if first < cols:
            gram[pl.ds(first, piece), :] = value
        else:
            projected[pl.ds(first - cols, piece), :] = value


def filter_kernel(
    n_row, n_col, send_rows, sources, holder, x_in, diagonal, dense_in,
    filtered, sum_in,
    dense, mask,
    x0, step_one, stacked, total, blocks, spread, upspread, out_buf, in_buf, gathered,
    piece_out, piece_in, sum_out,
    dense_sem,
    send_sem, recv_sem, col_send, col_recv, piece_send, piece_recv, sum_send, sum_recv,
):
    me = lax.axis_index("row")
    mine = lax.axis_index("col")
    cols, length = x_in.shape
    rows = length // B
    pairs = length // PAIR
    slots = 2 * n_row
    tiles = length // TILE
    bf16 = jnp.bfloat16
    f32 = jnp.float32

    barrier = pltpu.get_barrier_semaphore()
    for step in range(1, n_row):
        pl.semaphore_signal(barrier, inc=1, device_id={"row": lax.rem(me + step, n_row)}, device_id_type=MESH)
    for step in range(1, n_col):
        pl.semaphore_signal(barrier, inc=1, device_id={"col": lax.rem(mine + step, n_col)}, device_id_type=MESH)

    def dense_copy(tile):
        return pltpu.make_async_copy(dense_in.at[tile], dense.at[tile], dense_sem.at[tile])

    for tile in range(tiles):
        dense_copy(tile).start()

    def columns(at, width):
        return pl.ds(pl.multiple_of(at * width, width), width)

    low = lax.broadcasted_iota(jnp.int32, (cols, PAIR), 1) < B

    def both(values):
        turned = pltpu.roll(values, B, 1)
        return jnp.where(low, values, turned), jnp.where(low, turned, values)

    lane_block = lax.broadcasted_iota(jnp.int32, (1, length), 1) >> 6

    def mask_body(slot, carry):
        mask[pl.ds(slot, 1), :] = jnp.where(lane_block == send_rows[slot], 1.0, 0.0)
        return carry

    lax.fori_loop(0, slots, mask_body, 0)

    def keep_blocks(pair, values):
        first, second = both(values)
        blocks[2 * pair] = first.astype(bf16)
        blocks[2 * pair + 1] = second.astype(bf16)

    order = order_matrix()
    for tile in range(tiles):
        here = pl.ds(tile * TILE, TILE)
        value = dot(x_in[:, here], order, NN)
        x0[:, here] = value.astype(bf16)
        keep_blocks(2 * tile, value[:, :PAIR])
        keep_blocks(2 * tile + 1, value[:, PAIR:])

    upspread[slots] = jnp.zeros((cols, PAIR), f32)

    def arrived_at(row, slot):
        source = sources[slot, row]
        return upspread[jnp.where(source >= rows, source - rows, slots)]

    pl.semaphore_wait(barrier, n_row + n_col - 2)

    def row_copy(phase, slot_here, slot_there, peer):
        return pltpu.make_async_remote_copy(
            src_ref=out_buf.at[phase, slot_here],
            dst_ref=in_buf.at[phase, slot_there],
            send_sem=send_sem.at[phase, slot_here],
            recv_sem=recv_sem.at[phase, slot_there],
            device_id={"row": peer},
            device_id_type=MESH,
        )

    def pick(first, second):
        return jnp.where(low, blocks[first].astype(f32), blocks[second].astype(f32)).astype(bf16)

    def apply_operator(phase, source, finish, beside=None):
        for pack in range(slots // 4):
            at = 4 * pack
            near = jnp.concatenate([pick(holder[at], holder[at + 1]), pick(holder[at + 2], holder[at + 3])], 1)
            product = dot(near, diagonal[pack], NN).astype(bf16)
            for inner in range(2):
                peer = 2 * pack + inner
                out_buf[phase, peer, :, pl.ds(0, PAIR)] = pick(send_rows[2 * peer], send_rows[2 * peer + 1])
                out_buf[phase, peer, :, pl.ds(PAIR, PAIR)] = product[:, inner * PAIR : (inner + 1) * PAIR]
        for step in range(1, n_row):
            peer = lax.rem(me + step, n_row)
            row_copy(phase, peer, me, peer).start()
        in_buf[phase, me] = out_buf[phase, me]

        def local_body(tile, carry):
            if phase == 0:
                dense_copy(tile).wait()
            total[:, columns(tile, TILE)] = dot(source[...], dense[tile], NN)
            return carry

        lax.fori_loop(0, tiles, local_body, 0)
        for step in range(1, n_row):
            peer = lax.rem(me + step, n_row)
            row_copy(phase, peer, peer, peer).wait_recv()
        if beside is not None:
            beside()

        for pack in range(slots // 4):
            far = jnp.concatenate([in_buf[phase, 2 * pack + inner, :, pl.ds(0, PAIR)] for inner in range(2)], 1)
            product = dot(far, diagonal[pack], NT)
            for inner in range(2):
                peer = 2 * pack + inner
                first, second = both(product[:, inner * PAIR : (inner + 1) * PAIR])
                upspread[2 * peer] = first
                upspread[2 * peer + 1] = second
                first, second = both(in_buf[phase, peer, :, pl.ds(PAIR, PAIR)].astype(f32))
                spread[2 * peer] = first
                spread[2 * peer + 1] = second

        def finish_body(pair, carry):
            here = columns(pair, PAIR)
            value = total[:, here] + jnp.where(
                low,
                arrived_at(2 * pair, 1) + arrived_at(2 * pair, 2),
                arrived_at(2 * pair + 1, 1) + arrived_at(2 * pair + 1, 2),
            )
            for slot in range(slots):
                value = value + spread[slot] * mask[pl.ds(slot, 1), here]
            finish(pair, here, value)
            return carry

        lax.fori_loop(0, pairs, finish_body, 0)

    def first_finish(pair, here, value):
        new = ((value - center_value * x0[:, here].astype(f32)) / half_width).astype(bf16)
        step_one[:, here] = new
        keep_blocks(pair, new.astype(f32))

    def second_finish(pair, here, value):
        old = step_one[:, here].astype(f32)
        new = (2.0 * (value - center_value * old) / half_width - x0[:, here].astype(f32)).astype(bf16)
        stacked[pl.ds(0, cols), here] = new
        gathered[mine, :, here] = new
        filtered[:, here] = new
        keep_blocks(pair, new.astype(f32))

    def third_finish(pair, here, value):
        stacked[pl.ds(cols, cols), here] = value.astype(bf16)

    def col_copy(slot_here, slot_there, sem_at, peer):
        return pltpu.make_async_remote_copy(
            src_ref=gathered.at[slot_here],
            dst_ref=gathered.at[slot_there],
            send_sem=col_send.at[sem_at],
            recv_sem=col_recv.at[slot_there],
            device_id={"col": peer},
            device_id_type=MESH,
        )

    sibling = mine + 1 - 2 * lax.rem(mine, 2)
    across = [lax.rem(mine + 2 * step, n_col) for step in range(1, n_col // 2)]

    def start_gather():
        for at, peer in enumerate(across):
            col_copy(mine, mine, at, peer).start()
        col_copy(mine, mine, len(across), sibling).start()

    def forward_gather():
        for at, peer in enumerate(across):
            col_copy(peer, peer, at, peer).wait_recv()
            col_copy(peer, peer, len(across) + 1 + at, sibling).start()

    def end_gather():
        col_copy(sibling, sibling, 0, sibling).wait_recv()
        for peer in across:
            other = peer + 1 - 2 * lax.rem(peer, 2)
            col_copy(other, other, 0, sibling).wait_recv()

    apply_operator(0, x0, first_finish)
    apply_operator(1, step_one, second_finish)
    start_gather()
    apply_operator(2, stacked.at[pl.ds(0, cols)], third_finish, forward_gather)
    end_gather()

    piece = 2 * cols // n_row
    part = dot(stacked[...], gathered[...].reshape(n_col * cols, length), NT)
    for at in range(n_row):
        piece_out[at] = part[at * piece : (at + 1) * piece].astype(piece_out.dtype)

    def piece_copy(slot_here, slot_there, peer):
        return pltpu.make_async_remote_copy(
            src_ref=piece_out.at[slot_here],
            dst_ref=piece_in.at[slot_there],
            send_sem=piece_send.at[slot_here],
            recv_sem=piece_recv.at[slot_there],
            device_id={"row": peer},
            device_id_type=MESH,
        )

    def sum_copy(slot_there, peer):
        return pltpu.make_async_remote_copy(
            src_ref=sum_out,
            dst_ref=sum_in.at[slot_there],
            send_sem=sum_send.at[peer],
            recv_sem=sum_recv.at[slot_there],
            device_id={"row": peer},
            device_id_type=MESH,
        )

    peers = [lax.rem(me + step, n_row) for step in range(1, n_row)]
    for peer in peers:
        piece_copy(peer, me, peer).start()
    piece_in[me] = piece_out[me]
    for peer in peers:
        piece_copy(peer, peer, peer).wait_recv()
    summed = piece_in[0].astype(f32)
    for peer in range(1, n_row):
        summed = summed + piece_in[peer].astype(f32)
    sum_out[...] = summed.astype(sum_out.dtype)
    for peer in peers:
        sum_copy(me, peer).start()
    sum_in[me] = sum_out[...]
    for peer in peers:
        sum_copy(peer, peer).wait_recv()
    for peer in peers:
        for phase in range(3):
            row_copy(phase, peer, me, peer).wait_send()
        piece_copy(peer, me, peer).wait_send()
        sum_copy(me, peer).wait_send()
    for at, peer in enumerate(across):
        col_copy(mine, mine, at, peer).wait_send()
        col_copy(peer, peer, len(across) + 1 + at, sibling).wait_send()
    col_copy(mine, mine, len(across), sibling).wait_send()


def on_device(vectors, hblocks, counts, sources, send_rows):
    rows = hblocks.shape[0]
    cols, length = vectors.shape
    slots = send_rows.shape[0]
    n_row = lax.axis_size("row")
    n_col = lax.axis_size("col")
    assert slots == 2 * n_row
    named = rows + slots
    tiles = length // TILE
    total_cols = n_col * cols
    piece = 2 * cols // n_row
    sum_type = jnp.bfloat16 if piece % 16 == 0 else jnp.float32
    smem = pl.BlockSpec(memory_space=pltpu.SMEM)
    vmem = pl.BlockSpec(memory_space=pltpu.VMEM)
    dma = pltpu.SemaphoreType.DMA
    bf16 = jnp.bfloat16
    f32 = jnp.float32
    by_slot = sources.T
    place_steps = K // SLOTS_STEP
    dense, diagonal, holder = pl.pallas_call(
        functools.partial(build_kernel, rows, slots),
        grid=(place_steps + tiles // TILES_STEP,),
        out_shape=(
            jax.ShapeDtypeStruct((tiles, length, TILE), bf16),
            jax.ShapeDtypeStruct((slots // 4, TILE, TILE), bf16),
            jax.ShapeDtypeStruct((slots,), jnp.int32),
        ),
        in_specs=[smem, smem, pl.BlockSpec((SLOTS_STEP, rows, B * B), lambda step: (jnp.minimum(step, place_steps - 1), 0, 0))],
        out_specs=(
            pl.BlockSpec((TILES_STEP, length, TILE), lambda step: (jnp.maximum(step - place_steps, 0), 0, 0)),
            pl.BlockSpec((slots // 4, TILE, TILE), lambda step: (0, 0, 0)),
            smem,
        ),
        scratch_shapes=[
            pltpu.VMEM((TILE, TILE), bf16),
            pltpu.VMEM((TILE, TILE), bf16),
            pltpu.VMEM((TILE, TILE), bf16),
            pltpu.VMEM((2 * HALF * (rows + 8), PAIR), f32),
            pltpu.VMEM((rows, named // 2, B, PAIR), bf16),
        ],
        compiler_params=pltpu.CompilerParams(vmem_limit_bytes=56 * 1024 * 1024),
    )(by_slot, counts, hblocks.transpose(1, 0, 2))

    ordered, sums = pl.pallas_call(
        functools.partial(filter_kernel, n_row, n_col),
        out_shape=(
            jax.ShapeDtypeStruct((cols, length), bf16),
            jax.ShapeDtypeStruct((n_row, piece, total_cols), sum_type),
        ),
        in_specs=[smem, smem, smem, vmem, vmem, pl.BlockSpec(memory_space=pl.ANY)],
        out_specs=(vmem, vmem),
        scratch_shapes=[
            pltpu.VMEM((tiles, length, TILE), bf16),
            pltpu.VMEM((slots, length), f32),
            pltpu.VMEM((cols, length), bf16),
            pltpu.VMEM((cols, length), bf16),
            pltpu.VMEM((2 * cols, length), bf16),
            pltpu.VMEM((cols, length), f32),
            pltpu.VMEM((rows, cols, PAIR), bf16),
            pltpu.VMEM((slots, cols, PAIR), f32),
            pltpu.VMEM((slots + 1, cols, PAIR), f32),
            pltpu.VMEM((3, n_row, cols, 2 * PAIR), bf16),
            pltpu.VMEM((3, n_row, cols, 2 * PAIR), bf16),
            pltpu.VMEM((n_col, cols, length), bf16),
            pltpu.VMEM((n_row, piece, total_cols), sum_type),
            pltpu.VMEM((n_row, piece, total_cols), sum_type),
            pltpu.VMEM((piece, total_cols), sum_type),
            dma((tiles,)),
            dma((3, n_row)), dma((3, n_row)),
            dma((n_col,)), dma((n_col,)),
            dma((n_row,)), dma((n_row,)),
            dma((n_row,)), dma((n_row,)),
        ],
        compiler_params=pltpu.CompilerParams(
            collective_id=0, has_side_effects=True, vmem_limit_bytes=56 * 1024 * 1024
        ),
    )(send_rows, by_slot, holder, vectors, diagonal, dense)

    filtered, gram, projected = pl.pallas_call(
        functools.partial(output_kernel, cols),
        out_shape=(
            jax.ShapeDtypeStruct((cols, length), bf16),
            jax.ShapeDtypeStruct((cols, total_cols), f32),
            jax.ShapeDtypeStruct((cols, total_cols), f32),
        ),
        in_specs=[vmem, vmem],
        out_specs=(vmem, vmem, vmem),
    )(ordered, sums)
    return filtered, gram.T, projected.T


def solution(mesh):
    return jax.shard_map(
        on_device,
        mesh=mesh,
        in_specs=(P("col", "row"), P("row", None, None), P("row"), P("row", None), P("row")),
        out_specs=(P("col", "row"), P(None, "col"), P(None, "col")),
        check_vma=False,
    )
```

```python
import functools

import jax
import jax.numpy as jnp
from jax import lax
from jax.experimental import pallas as pl
from jax.experimental.pallas import tpu as pltpu
from jax.sharding import PartitionSpec as P

B = 64
K = 12
PAIR = 2 * B
TILE = 256
UNROLL = 8
ROWS_STEP = 16
HALF = B // 2

center_value = 0.25
half_width = 1.5

MESH = pl.DeviceIdType.MESH
NN = (((1,), (0,)), ((), ()))
NT = (((1,), (1,)), ((), ()))


def dot(a, b, dims):
    return lax.dot_general(a, b, dims, preferred_element_type=jnp.float32)


def order_matrix(turned=0):
    row_at = lax.broadcasted_iota(jnp.int32, (TILE, TILE), 0)
    col_at = lax.broadcasted_iota(jnp.int32, (TILE, TILE), 1)
    within = row_at & (B - 1)
    target = (row_at - within) + (within & 1) * HALF + (within >> 1)
    target = target ^ turned
    return jnp.where(target == col_at, 1.0, 0.0).astype(jnp.bfloat16)


def build_kernel(rows, sources, counts, h, upper, diagonal, holder, order, order_turned, placed, remote):
    step = pl.program_id(0)
    here = upper.shape[0]
    slots = remote.shape[0]
    stride = here + 8
    size = HALF * stride
    first_row = step * here
    bf16 = jnp.bfloat16

    @pl.when(step == 0)
    def _():
        order[...] = order_matrix()
        order_turned[...] = order_matrix(B)

    def clear_body(row, carry):
        upper[row] = jnp.zeros_like(upper[row])
        return carry

    lax.fori_loop(0, here, clear_body, 0)
    pieces = B * B // TILE
    side = lax.broadcasted_iota(jnp.int32, (HALF, PAIR), 1) >> 6

    def slot_body(slot, carry):
        lanes = jnp.concatenate([h[slot, :, at * TILE : (at + 1) * TILE] for at in range(pieces)], 0)
        for turned, matrix in enumerate((order, order_turned)):
            value = dot(lanes, matrix[...], NN)
            for at in range(pieces):
                part = value[at * here : (at + 1) * here]
                placed[pl.ds(turned * size + 2 * at * stride, here), :] = part[:, :PAIR]
                placed[pl.ds(turned * size + (2 * at + 1) * stride, here), :] = part[:, PAIR:]

        def add_body(group, carry):
            news = []
            for inner in range(UNROLL):
                row = group * UNROLL + inner
                source = sources[slot, first_row + row]
                half = source & 1
                keep = side == jnp.where(slot < counts[first_row + row], half, 2)
                even = placed[pl.ds(half * size + row, HALF, stride=stride), :]
                odd = placed[pl.ds((1 - half) * size + row, HALF, stride=stride), :]
                even = jnp.where(keep, even, 0.0).astype(bf16)
                odd = jnp.where(keep, odd, 0.0).astype(bf16)
                old = upper[row, source >> 1]
                news.append((row, source >> 1, old + jnp.concatenate([even, odd], 0)))
            for row, pair, new in news:
                upper[row, pair] = new
            return carry

        return lax.fori_loop(0, here // UNROLL, add_body, carry)

    lax.fori_loop(0, K, slot_body, 0)
    block_side = lax.broadcasted_iota(jnp.int32, (B, PAIR), 1) >> 6

    def remote_body(row, carry):
        for slot in (1, 2):
            source = sources[slot, first_row + row]

            @pl.when(source >= rows)
            def _():
                holder[source - rows] = first_row + row
                value = upper[row, source >> 1].astype(jnp.float32)
                remote[source - rows] = jnp.where(block_side == (source & 1), value, 0.0).astype(bf16)

        return carry

    lax.fori_loop(0, here, remote_body, 0)

    @pl.when(step == pl.num_programs(0) - 1)
    def _():
        diagonal[...] = jnp.zeros_like(diagonal)
        for slot in range(slots):
            part = slot % 4
            diagonal[slot // 4, pl.ds(part * B, B), pl.ds((part // 2) * PAIR, PAIR)] = remote[slot]


def output_kernel(cols, ordered, sums, filtered, gram, projected):
    order = order_matrix()
    for tile in range(ordered.shape[1] // TILE):
        here = pl.ds(tile * TILE, TILE)
        filtered[:, here] = dot(ordered[:, here], order, NT).astype(jnp.bfloat16)
    count, piece = sums.shape[0], sums.shape[1]
    for at in range(count):
        value = sums[at].astype(jnp.float32)
        first = at * piece
        if first < cols:
            gram[pl.ds(first, piece), :] = value
        else:
            projected[pl.ds(first - cols, piece), :] = value


def filter_kernel(
    n_row, n_col, send_rows, sources, holder, x_in, diagonal, dense_in,
    filtered, sum_in,
    dense, mask,
    x0, step_one, stacked, total, blocks, spread, upspread, out_buf, in_buf, gathered,
    piece_out, piece_in, sum_out,
    dense_sem,
    send_sem, recv_sem, col_send, col_recv, piece_send, piece_recv, sum_send, sum_recv,
):
    me = lax.axis_index("row")
    mine = lax.axis_index("col")
    cols, length = x_in.shape
    rows = length // B
    pairs = length // PAIR
    slots = 2 * n_row
    tiles = length // TILE
    per_tile = TILE // B
    bf16 = jnp.bfloat16
    f32 = jnp.float32

    barrier = pltpu.get_barrier_semaphore()
    for step in range(1, n_row):
        pl.semaphore_signal(barrier, inc=1, device_id={"row": lax.rem(me + step, n_row)}, device_id_type=MESH)
    for step in range(1, n_col):
        pl.semaphore_signal(barrier, inc=1, device_id={"col": lax.rem(mine + step, n_col)}, device_id_type=MESH)

    def dense_copy(tile):
        here = pl.ds(tile * per_tile, per_tile)
        return pltpu.make_async_copy(
            dense_in.at[here, pl.ds(0, pairs)], dense.at[here], dense_sem.at[tile]
        )

    for tile in range(tiles):
        dense_copy(tile).start()

    def columns(at, width):
        return pl.ds(pl.multiple_of(at * width, width), width)

    low = lax.broadcasted_iota(jnp.int32, (cols, PAIR), 1) < B

    def both(values):
        turned = pltpu.roll(values, B, 1)
        return jnp.where(low, values, turned), jnp.where(low, turned, values)

    lane_block = lax.broadcasted_iota(jnp.int32, (1, length), 1) >> 6

    def mask_body(slot, carry):
        mask[pl.ds(slot, 1), :] = jnp.where(lane_block == send_rows[slot], 1.0, 0.0)
        return carry

    lax.fori_loop(0, slots, mask_body, 0)

    def keep_blocks(pair, values):
        first, second = both(values)
        blocks[2 * pair] = first.astype(bf16)
        blocks[2 * pair + 1] = second.astype(bf16)

    order = order_matrix()
    for tile in range(tiles):
        here = pl.ds(tile * TILE, TILE)
        value = dot(x_in[:, here], order, NN)
        x0[:, here] = value.astype(bf16)
        keep_blocks(2 * tile, value[:, :PAIR])
        keep_blocks(2 * tile + 1, value[:, PAIR:])

    upspread[slots] = jnp.zeros((cols, PAIR), f32)

    def arrived_at(row, slot):
        source = sources[slot, row]
        return upspread[jnp.where(source >= rows, source - rows, slots)]

    pl.semaphore_wait(barrier, n_row + n_col - 2)

    def row_copy(phase, slot_here, slot_there, peer):
        return pltpu.make_async_remote_copy(
            src_ref=out_buf.at[phase, slot_here],
            dst_ref=in_buf.at[phase, slot_there],
            send_sem=send_sem.at[phase, slot_here],
            recv_sem=recv_sem.at[phase, slot_there],
            device_id={"row": peer},
            device_id_type=MESH,
        )

    def pick(first, second):
        return jnp.where(low, blocks[first].astype(f32), blocks[second].astype(f32)).astype(bf16)

    def apply_operator(phase, source, finish, beside=None):
        for pack in range(slots // 4):
            at = 4 * pack
            near = jnp.concatenate([pick(holder[at], holder[at + 1]), pick(holder[at + 2], holder[at + 3])], 1)
            product = dot(near, diagonal[pack], NN).astype(bf16)
            for inner in range(2):
                peer = 2 * pack + inner
                out_buf[phase, peer, :, pl.ds(0, PAIR)] = pick(send_rows[2 * peer], send_rows[2 * peer + 1])
                out_buf[phase, peer, :, pl.ds(PAIR, PAIR)] = product[:, inner * PAIR : (inner + 1) * PAIR]
        for step in range(1, n_row):
            peer = lax.rem(me + step, n_row)
            row_copy(phase, peer, me, peer).start()
        in_buf[phase, me] = out_buf[phase, me]

        def local_body(tile, carry):
            down = jnp.concatenate([dense[:, 2 * tile + side].reshape(length, PAIR) for side in range(2)], 1)
            along = jnp.concatenate(
                [dense[pl.ds(tile * per_tile, per_tile), pair].reshape(TILE, PAIR) for pair in range(pairs)], 1
            )
            total[:, columns(tile, TILE)] = dot(source[...], down, NN) + dot(source[...], along, NT)
            return carry

        if phase == 0:
            for tile in range(tiles):
                dense_copy(tile).wait()

        lax.fori_loop(0, tiles, local_body, 0)
        for step in range(1, n_row):
            peer = lax.rem(me + step, n_row)
            row_copy(phase, peer, peer, peer).wait_recv()
        if beside is not None:
            beside()

        for pack in range(slots // 4):
            far = jnp.concatenate([in_buf[phase, 2 * pack + inner, :, pl.ds(0, PAIR)] for inner in range(2)], 1)
            product = dot(far, diagonal[pack], NT)
            for inner in range(2):
                peer = 2 * pack + inner
                first, second = both(product[:, inner * PAIR : (inner + 1) * PAIR])
                upspread[2 * peer] = first
                upspread[2 * peer + 1] = second
                first, second = both(in_buf[phase, peer, :, pl.ds(PAIR, PAIR)].astype(f32))
                spread[2 * peer] = first
                spread[2 * peer + 1] = second

        def finish_body(pair, carry):
            here = columns(pair, PAIR)
            value = total[:, here] + jnp.where(
                low,
                arrived_at(2 * pair, 1) + arrived_at(2 * pair, 2),
                arrived_at(2 * pair + 1, 1) + arrived_at(2 * pair + 1, 2),
            )
            for slot in range(slots):
                value = value + spread[slot] * mask[pl.ds(slot, 1), here]
            finish(pair, here, value)
            return carry

        lax.fori_loop(0, pairs, finish_body, 0)

    def first_finish(pair, here, value):
        new = ((value - center_value * x0[:, here].astype(f32)) / half_width).astype(bf16)
        step_one[:, here] = new
        keep_blocks(pair, new.astype(f32))

    def second_finish(pair, here, value):
        old = step_one[:, here].astype(f32)
        new = (2.0 * (value - center_value * old) / half_width - x0[:, here].astype(f32)).astype(bf16)
        stacked[pl.ds(0, cols), here] = new
        gathered[mine, :, here] = new
        filtered[:, here] = new
        keep_blocks(pair, new.astype(f32))

    def third_finish(pair, here, value):
        stacked[pl.ds(cols, cols), here] = value.astype(bf16)

    def col_copy(slot_here, slot_there, sem_at, peer):
        return pltpu.make_async_remote_copy(
            src_ref=gathered.at[slot_here],
            dst_ref=gathered.at[slot_there],
            send_sem=col_send.at[sem_at],
            recv_sem=col_recv.at[slot_there],
            device_id={"col": peer},
            device_id_type=MESH,
        )

    sibling = mine + 1 - 2 * lax.rem(mine, 2)
    across = [lax.rem(mine + 2 * step, n_col) for step in range(1, n_col // 2)]

    def start_gather():
        for at, peer in enumerate(across):
            col_copy(mine, mine, at, peer).start()
        col_copy(mine, mine, len(across), sibling).start()

    def forward_gather():
        for at, peer in enumerate(across):
            col_copy(peer, peer, at, peer).wait_recv()
            col_copy(peer, peer, len(across) + 1 + at, sibling).start()

    def end_gather():
        col_copy(sibling, sibling, 0, sibling).wait_recv()
        for peer in across:
            other = peer + 1 - 2 * lax.rem(peer, 2)
            col_copy(other, other, 0, sibling).wait_recv()

    apply_operator(0, x0, first_finish)
    apply_operator(1, step_one, second_finish)
    start_gather()
    apply_operator(2, stacked.at[pl.ds(0, cols)], third_finish, forward_gather)
    end_gather()

    piece = 2 * cols // n_row
    part = dot(stacked[...], gathered[...].reshape(n_col * cols, length), NT)
    for at in range(n_row):
        piece_out[at] = part[at * piece : (at + 1) * piece].astype(piece_out.dtype)

    def piece_copy(slot_here, slot_there, peer):
        return pltpu.make_async_remote_copy(
            src_ref=piece_out.at[slot_here],
            dst_ref=piece_in.at[slot_there],
            send_sem=piece_send.at[slot_here],
            recv_sem=piece_recv.at[slot_there],
            device_id={"row": peer},
            device_id_type=MESH,
        )

    def sum_copy(slot_there, peer):
        return pltpu.make_async_remote_copy(
            src_ref=sum_out,
            dst_ref=sum_in.at[slot_there],
            send_sem=sum_send.at[peer],
            recv_sem=sum_recv.at[slot_there],
            device_id={"row": peer},
            device_id_type=MESH,
        )

    peers = [lax.rem(me + step, n_row) for step in range(1, n_row)]
    for peer in peers:
        piece_copy(peer, me, peer).start()
    piece_in[me] = piece_out[me]
    for peer in peers:
        piece_copy(peer, peer, peer).wait_recv()
    summed = piece_in[0].astype(f32)
    for peer in range(1, n_row):
        summed = summed + piece_in[peer].astype(f32)
    sum_out[...] = summed.astype(sum_out.dtype)
    for peer in peers:
        sum_copy(me, peer).start()
    sum_in[me] = sum_out[...]
    for peer in peers:
        sum_copy(peer, peer).wait_recv()
    for peer in peers:
        for phase in range(3):
            row_copy(phase, peer, me, peer).wait_send()
        piece_copy(peer, me, peer).wait_send()
        sum_copy(me, peer).wait_send()
    for at, peer in enumerate(across):
        col_copy(mine, mine, at, peer).wait_send()
        col_copy(peer, peer, len(across) + 1 + at, sibling).wait_send()
    col_copy(mine, mine, len(across), sibling).wait_send()


def on_device(vectors, hblocks, counts, sources, send_rows):
    rows = hblocks.shape[0]
    cols, length = vectors.shape
    slots = send_rows.shape[0]
    n_row = lax.axis_size("row")
    n_col = lax.axis_size("col")
    assert slots == 2 * n_row
    named = rows + slots
    tiles = length // TILE
    total_cols = n_col * cols
    piece = 2 * cols // n_row
    sum_type = jnp.bfloat16 if piece % 16 == 0 else jnp.float32
    smem = pl.BlockSpec(memory_space=pltpu.SMEM)
    vmem = pl.BlockSpec(memory_space=pltpu.VMEM)
    dma = pltpu.SemaphoreType.DMA
    bf16 = jnp.bfloat16
    f32 = jnp.float32
    by_slot = sources.T
    upper, diagonal, holder = pl.pallas_call(
        functools.partial(build_kernel, rows),
        grid=(rows // ROWS_STEP,),
        out_shape=(
            jax.ShapeDtypeStruct((rows, named // 2, B, PAIR), bf16),
            jax.ShapeDtypeStruct((slots // 4, TILE, TILE), bf16),
            jax.ShapeDtypeStruct((slots,), jnp.int32),
        ),
        in_specs=[smem, smem, pl.BlockSpec((K, ROWS_STEP, B * B), lambda step: (0, step, 0))],
        out_specs=(
            pl.BlockSpec((ROWS_STEP, named // 2, B, PAIR), lambda step: (step, 0, 0, 0)),
            pl.BlockSpec((slots // 4, TILE, TILE), lambda step: (0, 0, 0)),
            smem,
        ),
        scratch_shapes=[
            pltpu.VMEM((TILE, TILE), bf16),
            pltpu.VMEM((TILE, TILE), bf16),
            pltpu.VMEM((2 * HALF * (ROWS_STEP + 8), PAIR), f32),
            pltpu.VMEM((slots, B, PAIR), bf16),
        ],
        compiler_params=pltpu.CompilerParams(vmem_limit_bytes=56 * 1024 * 1024),
    )(by_slot, counts, hblocks.transpose(1, 0, 2))

    ordered, sums = pl.pallas_call(
        functools.partial(filter_kernel, n_row, n_col),
        out_shape=(
            jax.ShapeDtypeStruct((cols, length), bf16),
            jax.ShapeDtypeStruct((n_row, piece, total_cols), sum_type),
        ),
        in_specs=[smem, smem, smem, vmem, vmem, pl.BlockSpec(memory_space=pl.ANY)],
        out_specs=(vmem, vmem),
        scratch_shapes=[
            pltpu.VMEM((rows, length // PAIR, B, PAIR), bf16),
            pltpu.VMEM((slots, length), f32),
            pltpu.VMEM((cols, length), bf16),
            pltpu.VMEM((cols, length), bf16),
            pltpu.VMEM((2 * cols, length), bf16),
            pltpu.VMEM((cols, length), f32),
            pltpu.VMEM((rows, cols, PAIR), bf16),
            pltpu.VMEM((slots, cols, PAIR), f32),
            pltpu.VMEM((slots + 1, cols, PAIR), f32),
            pltpu.VMEM((3, n_row, cols, 2 * PAIR), bf16),
            pltpu.VMEM((3, n_row, cols, 2 * PAIR), bf16),
            pltpu.VMEM((n_col, cols, length), bf16),
            pltpu.VMEM((n_row, piece, total_cols), sum_type),
            pltpu.VMEM((n_row, piece, total_cols), sum_type),
            pltpu.VMEM((piece, total_cols), sum_type),
            dma((tiles,)),
            dma((3, n_row)), dma((3, n_row)),
            dma((n_col,)), dma((n_col,)),
            dma((n_row,)), dma((n_row,)),
            dma((n_row,)), dma((n_row,)),
        ],
        compiler_params=pltpu.CompilerParams(
            collective_id=0, has_side_effects=True, vmem_limit_bytes=56 * 1024 * 1024
        ),
    )(send_rows, by_slot, holder, vectors, diagonal, upper)

    filtered, gram, projected = pl.pallas_call(
        functools.partial(output_kernel, cols),
        out_shape=(
            jax.ShapeDtypeStruct((cols, length), bf16),
            jax.ShapeDtypeStruct((cols, total_cols), f32),
            jax.ShapeDtypeStruct((cols, total_cols), f32),
        ),
        in_specs=[vmem, vmem],
        out_specs=(vmem, vmem, vmem),
    )(ordered, sums)
    return filtered, gram.T, projected.T


def solution(mesh):
    return jax.shard_map(
        on_device,
        mesh=mesh,
        in_specs=(P("col", "row"), P("row", None, None), P("row"), P("row", None), P("row")),
        out_specs=(P("col", "row"), P(None, "col"), P(None, "col")),
        check_vma=False,
    )
```

```python
import functools

import jax
import jax.numpy as jnp
from jax import lax
from jax.experimental import pallas as pl
from jax.experimental.pallas import tpu as pltpu
from jax.sharding import PartitionSpec as P

B = 64
K = 12
PAIR = 2 * B
TILE = 256
UNROLL = 8
ROWS_STEP = 16
HALF = B // 2

center_value = 0.25
half_width = 1.5

MESH = pl.DeviceIdType.MESH
NN = (((1,), (0,)), ((), ()))
NT = (((1,), (1,)), ((), ()))


def dot(a, b, dims):
    return lax.dot_general(a, b, dims, preferred_element_type=jnp.float32)


def order_matrix(turned=0):
    row_at = lax.broadcasted_iota(jnp.int32, (TILE, TILE), 0)
    col_at = lax.broadcasted_iota(jnp.int32, (TILE, TILE), 1)
    within = row_at & (B - 1)
    target = (row_at - within) + (within & 1) * HALF + ((within >> 1) & 1) * (HALF // 2) + (within >> 2)
    target = target ^ turned
    return jnp.where(target == col_at, 1.0, 0.0).astype(jnp.bfloat16)


def build_kernel(rows, sources, counts, h, upper, diagonal, holder, order, swap, marks, placed, remote):
    step = pl.program_id(0)
    here = upper.shape[0]
    slots = remote.shape[0]
    pieces = B * B // TILE
    first_row = step * here
    bf16 = jnp.bfloat16

    @pl.when(step == 0)
    def _():
        order[:, pl.ds(0, TILE)] = order_matrix()
        order[:, pl.ds(TILE, TILE)] = order_matrix(B)
        row_at = lax.broadcasted_iota(jnp.int32, (TILE, TILE), 0)
        col_at = lax.broadcasted_iota(jnp.int32, (TILE, TILE), 1)
        swap[...] = jnp.where(col_at == (row_at & (pieces - 1)) * here + (row_at >> 4), 1.0, 0.0).astype(bf16)
        side = lax.broadcasted_iota(jnp.int32, (here, PAIR), 1) >> 6
        for wanted in range(3):
            marks[wanted] = jnp.where(side == wanted, 1.0, 0.0).astype(bf16)

    def clear_body(row, carry):
        upper[row] = jnp.zeros_like(upper[row])
        return carry

    lax.fori_loop(0, here, clear_body, 0)

    def order_body(pack, carry):
        for inner in range(2):
            slot = 2 * pack + inner
            lanes = jnp.concatenate([h[slot, :, at * TILE : (at + 1) * TILE] for at in range(pieces)], 0)
            swapped = dot(swap[...], lanes, NN).astype(bf16)
            value = dot(swapped, order[...], NN).astype(bf16)
            for turned in range(2):
                for part in range(2):
                    at = (2 * turned + part) * PAIR
                    placed[slot, turned, part] = value[:, at : at + PAIR].reshape(here, pieces, PAIR)
        return carry

    lax.fori_loop(0, K // 2, order_body, 0)

    def add_body(slot, carry):
        for group in range(here // UNROLL):
            news = []
            for row in range(group * UNROLL, (group + 1) * UNROLL):
                source = sources[slot, first_row + row]
                half = source & 1
                mark = marks[jnp.where(slot < counts[first_row + row], half, 2)]
                blocks = [
                    placed[slot, turned, part, row] * mark
                    for turned in (half, 1 - half)
                    for part in range(2)
                ]
                old = upper[row, source >> 1]
                news.append((row, source >> 1, old + jnp.concatenate(blocks, 0)))
            for row, pair, new in news:
                upper[row, pair] = new
        return carry

    lax.fori_loop(0, K, add_body, 0)
    block_side = lax.broadcasted_iota(jnp.int32, (B, PAIR), 1) >> 6

    def remote_body(row, carry):
        for slot in (1, 2):
            source = sources[slot, first_row + row]

            @pl.when(source >= rows)
            def _():
                holder[source - rows] = first_row + row
                value = upper[row, source >> 1].astype(jnp.float32)
                remote[source - rows] = jnp.where(block_side == (source & 1), value, 0.0).astype(bf16)

        return carry

    lax.fori_loop(0, here, remote_body, 0)

    @pl.when(step == pl.num_programs(0) - 1)
    def _():
        diagonal[...] = jnp.zeros_like(diagonal)
        for slot in range(slots):
            part = slot % 4
            diagonal[slot // 4, pl.ds(part * B, B), pl.ds((part // 2) * PAIR, PAIR)] = remote[slot]


def output_kernel(cols, ordered, sums, filtered, gram, projected):
    order = order_matrix()
    for tile in range(ordered.shape[1] // TILE):
        here = pl.ds(tile * TILE, TILE)
        filtered[:, here] = dot(ordered[:, here], order, NT).astype(jnp.bfloat16)
    count, piece = sums.shape[0], sums.shape[1]
    for at in range(count):
        value = sums[at].astype(jnp.float32)
        first = at * piece
        if first < cols:
            gram[pl.ds(first, piece), :] = value
        else:
            projected[pl.ds(first - cols, piece), :] = value


def filter_kernel(
    n_row, n_col, send_rows, sources, holder, x_in, diagonal, dense_in,
    filtered, sum_in,
    dense, mask,
    x0, step_one, stacked, total, blocks, spread, upspread, out_buf, in_buf, gathered,
    piece_out, piece_in, sum_out,
    dense_sem,
    send_sem, recv_sem, col_send, col_recv, piece_send, piece_recv, sum_send, sum_recv,
):
    me = lax.axis_index("row")
    mine = lax.axis_index("col")
    cols, length = x_in.shape
    rows = length // B
    pairs = length // PAIR
    slots = 2 * n_row
    tiles = length // TILE
    per_tile = TILE // B
    bf16 = jnp.bfloat16
    f32 = jnp.float32

    barrier = pltpu.get_barrier_semaphore()
    for step in range(1, n_row):
        pl.semaphore_signal(barrier, inc=1, device_id={"row": lax.rem(me + step, n_row)}, device_id_type=MESH)
    for step in range(1, n_col):
        pl.semaphore_signal(barrier, inc=1, device_id={"col": lax.rem(mine + step, n_col)}, device_id_type=MESH)

    def dense_copy(tile):
        here = pl.ds(tile * per_tile, per_tile)
        return pltpu.make_async_copy(
            dense_in.at[here, pl.ds(0, pairs)], dense.at[here], dense_sem.at[tile]
        )

    for tile in range(tiles):
        dense_copy(tile).start()

    def columns(at, width):
        return pl.ds(pl.multiple_of(at * width, width), width)

    low = lax.broadcasted_iota(jnp.int32, (cols, PAIR), 1) < B

    def both(values):
        turned = pltpu.roll(values, B, 1)
        return jnp.where(low, values, turned), jnp.where(low, turned, values)

    lane_block = lax.broadcasted_iota(jnp.int32, (1, length), 1) >> 6

    def mask_body(slot, carry):
        mask[pl.ds(slot, 1), :] = jnp.where(lane_block == send_rows[slot], 1.0, 0.0)
        return carry

    lax.fori_loop(0, slots, mask_body, 0)

    def keep_blocks(pair, values):
        first, second = both(values)
        blocks[2 * pair] = first.astype(bf16)
        blocks[2 * pair + 1] = second.astype(bf16)

    order = order_matrix()
    for tile in range(tiles):
        here = pl.ds(tile * TILE, TILE)
        value = dot(x_in[:, here], order, NN)
        x0[:, here] = value.astype(bf16)
        keep_blocks(2 * tile, value[:, :PAIR])
        keep_blocks(2 * tile + 1, value[:, PAIR:])

    upspread[slots] = jnp.zeros((cols, PAIR), f32)

    def arrived_at(row, slot):
        source = sources[slot, row]
        return upspread[jnp.where(source >= rows, source - rows, slots)]

    pl.semaphore_wait(barrier, n_row + n_col - 2)

    def row_copy(phase, slot_here, slot_there, peer):
        return pltpu.make_async_remote_copy(
            src_ref=out_buf.at[phase, slot_here],
            dst_ref=in_buf.at[phase, slot_there],
            send_sem=send_sem.at[phase, slot_here],
            recv_sem=recv_sem.at[phase, slot_there],
            device_id={"row": peer},
            device_id_type=MESH,
        )

    def pick(first, second):
        return jnp.where(low, blocks[first].astype(f32), blocks[second].astype(f32)).astype(bf16)

    def apply_operator(phase, source, finish, beside=None):
        for pack in range(slots // 4):
            at = 4 * pack
            near = jnp.concatenate([pick(holder[at], holder[at + 1]), pick(holder[at + 2], holder[at + 3])], 1)
            product = dot(near, diagonal[pack], NN).astype(bf16)
            for inner in range(2):
                peer = 2 * pack + inner
                out_buf[phase, peer, :, pl.ds(0, PAIR)] = pick(send_rows[2 * peer], send_rows[2 * peer + 1])
                out_buf[phase, peer, :, pl.ds(PAIR, PAIR)] = product[:, inner * PAIR : (inner + 1) * PAIR]
        for step in range(1, n_row):
            peer = lax.rem(me + step, n_row)
            row_copy(phase, peer, me, peer).start()
        in_buf[phase, me] = out_buf[phase, me]

        def local_body(tile, carry):
            down = jnp.concatenate([dense[:, 2 * tile + side].reshape(length, PAIR) for side in range(2)], 1)
            along = jnp.concatenate(
                [dense[pl.ds(tile * per_tile, per_tile), pair].reshape(TILE, PAIR) for pair in range(pairs)], 1
            )
            total[:, columns(tile, TILE)] = dot(source[...], down, NN) + dot(source[...], along, NT)
            return carry

        if phase == 0:
            for tile in range(tiles):
                dense_copy(tile).wait()

        lax.fori_loop(0, tiles, local_body, 0)
        for step in range(1, n_row):
            peer = lax.rem(me + step, n_row)
            row_copy(phase, peer, peer, peer).wait_recv()
        if beside is not None:
            beside()

        for pack in range(slots // 4):
            far = jnp.concatenate([in_buf[phase, 2 * pack + inner, :, pl.ds(0, PAIR)] for inner in range(2)], 1)
            product = dot(far, diagonal[pack], NT)
            for inner in range(2):
                peer = 2 * pack + inner
                first, second = both(product[:, inner * PAIR : (inner + 1) * PAIR])
                upspread[2 * peer] = first
                upspread[2 * peer + 1] = second
                first, second = both(in_buf[phase, peer, :, pl.ds(PAIR, PAIR)].astype(f32))
                spread[2 * peer] = first
                spread[2 * peer + 1] = second

        def finish_body(pair, carry):
            here = columns(pair, PAIR)
            value = total[:, here] + jnp.where(
                low,
                arrived_at(2 * pair, 1) + arrived_at(2 * pair, 2),
                arrived_at(2 * pair + 1, 1) + arrived_at(2 * pair + 1, 2),
            )
            for slot in range(slots):
                value = value + spread[slot] * mask[pl.ds(slot, 1), here]
            finish(pair, here, value)
            return carry

        lax.fori_loop(0, pairs, finish_body, 0)

    def first_finish(pair, here, value):
        new = ((value - center_value * x0[:, here].astype(f32)) / half_width).astype(bf16)
        step_one[:, here] = new
        keep_blocks(pair, new.astype(f32))

    def second_finish(pair, here, value):
        old = step_one[:, here].astype(f32)
        new = (2.0 * (value - center_value * old) / half_width - x0[:, here].astype(f32)).astype(bf16)
        stacked[pl.ds(0, cols), here] = new
        gathered[mine, :, here] = new
        filtered[:, here] = new
        keep_blocks(pair, new.astype(f32))

    def third_finish(pair, here, value):
        stacked[pl.ds(cols, cols), here] = value.astype(bf16)

    def col_copy(slot_here, slot_there, sem_at, peer):
        return pltpu.make_async_remote_copy(
            src_ref=gathered.at[slot_here],
            dst_ref=gathered.at[slot_there],
            send_sem=col_send.at[sem_at],
            recv_sem=col_recv.at[slot_there],
            device_id={"col": peer},
            device_id_type=MESH,
        )

    sibling = mine + 1 - 2 * lax.rem(mine, 2)
    across = [lax.rem(mine + 2 * step, n_col) for step in range(1, n_col // 2)]

    def start_gather():
        for at, peer in enumerate(across):
            col_copy(mine, mine, at, peer).start()
        col_copy(mine, mine, len(across), sibling).start()

    def forward_gather():
        for at, peer in enumerate(across):
            col_copy(peer, peer, at, peer).wait_recv()
            col_copy(peer, peer, len(across) + 1 + at, sibling).start()

    def end_gather():
        col_copy(sibling, sibling, 0, sibling).wait_recv()
        for peer in across:
            other = peer + 1 - 2 * lax.rem(peer, 2)
            col_copy(other, other, 0, sibling).wait_recv()

    apply_operator(0, x0, first_finish)
    apply_operator(1, step_one, second_finish)
    start_gather()
    apply_operator(2, stacked.at[pl.ds(0, cols)], third_finish, forward_gather)
    end_gather()

    piece = 2 * cols // n_row
    part = dot(stacked[...], gathered[...].reshape(n_col * cols, length), NT)
    for at in range(n_row):
        piece_out[at] = part[at * piece : (at + 1) * piece].astype(piece_out.dtype)

    def piece_copy(slot_here, slot_there, peer):
        return pltpu.make_async_remote_copy(
            src_ref=piece_out.at[slot_here],
            dst_ref=piece_in.at[slot_there],
            send_sem=piece_send.at[slot_here],
            recv_sem=piece_recv.at[slot_there],
            device_id={"row": peer},
            device_id_type=MESH,
        )

    def sum_copy(slot_there, peer):
        return pltpu.make_async_remote_copy(
            src_ref=sum_out,
            dst_ref=sum_in.at[slot_there],
            send_sem=sum_send.at[peer],
            recv_sem=sum_recv.at[slot_there],
            device_id={"row": peer},
            device_id_type=MESH,
        )

    peers = [lax.rem(me + step, n_row) for step in range(1, n_row)]
    for peer in peers:
        piece_copy(peer, me, peer).start()
    piece_in[me] = piece_out[me]
    for peer in peers:
        piece_copy(peer, peer, peer).wait_recv()
    summed = piece_in[0].astype(f32)
    for peer in range(1, n_row):
        summed = summed + piece_in[peer].astype(f32)
    sum_out[...] = summed.astype(sum_out.dtype)
    for peer in peers:
        sum_copy(me, peer).start()
    sum_in[me] = sum_out[...]
    for peer in peers:
        sum_copy(peer, peer).wait_recv()
    for peer in peers:
        for phase in range(3):
            row_copy(phase, peer, me, peer).wait_send()
        piece_copy(peer, me, peer).wait_send()
        sum_copy(me, peer).wait_send()
    for at, peer in enumerate(across):
        col_copy(mine, mine, at, peer).wait_send()
        col_copy(peer, peer, len(across) + 1 + at, sibling).wait_send()
    col_copy(mine, mine, len(across), sibling).wait_send()


def on_device(vectors, hblocks, counts, sources, send_rows):
    rows = hblocks.shape[0]
    cols, length = vectors.shape
    slots = send_rows.shape[0]
    n_row = lax.axis_size("row")
    n_col = lax.axis_size("col")
    assert slots == 2 * n_row
    named = rows + slots
    tiles = length // TILE
    total_cols = n_col * cols
    piece = 2 * cols // n_row
    sum_type = jnp.bfloat16 if piece % 16 == 0 else jnp.float32
    smem = pl.BlockSpec(memory_space=pltpu.SMEM)
    vmem = pl.BlockSpec(memory_space=pltpu.VMEM)
    dma = pltpu.SemaphoreType.DMA
    bf16 = jnp.bfloat16
    f32 = jnp.float32
    by_slot = sources.T
    upper, diagonal, holder = pl.pallas_call(
        functools.partial(build_kernel, rows),
        grid=(rows // ROWS_STEP,),
        out_shape=(
            jax.ShapeDtypeStruct((rows, named // 2, B, PAIR), bf16),
            jax.ShapeDtypeStruct((slots // 4, TILE, TILE), bf16),
            jax.ShapeDtypeStruct((slots,), jnp.int32),
        ),
        in_specs=[smem, smem, pl.BlockSpec((K, ROWS_STEP, B * B), lambda step: (0, step, 0))],
        out_specs=(
            pl.BlockSpec((ROWS_STEP, named // 2, B, PAIR), lambda step: (step, 0, 0, 0)),
            pl.BlockSpec((slots // 4, TILE, TILE), lambda step: (0, 0, 0)),
            smem,
        ),
        scratch_shapes=[
            pltpu.VMEM((TILE, 2 * TILE), bf16),
            pltpu.VMEM((TILE, TILE), bf16),
            pltpu.VMEM((3, ROWS_STEP, PAIR), bf16),
            pltpu.VMEM((K, 2, 2, ROWS_STEP, B * B // TILE, PAIR), bf16),
            pltpu.VMEM((slots, B, PAIR), bf16),
        ],
        compiler_params=pltpu.CompilerParams(vmem_limit_bytes=56 * 1024 * 1024),
    )(by_slot, counts, hblocks.transpose(1, 0, 2))

    ordered, sums = pl.pallas_call(
        functools.partial(filter_kernel, n_row, n_col),
        out_shape=(
            jax.ShapeDtypeStruct((cols, length), bf16),
            jax.ShapeDtypeStruct((n_row, piece, total_cols), sum_type),
        ),
        in_specs=[smem, smem, smem, vmem, vmem, pl.BlockSpec(memory_space=pl.ANY)],
        out_specs=(vmem, vmem),
        scratch_shapes=[
            pltpu.VMEM((rows, length // PAIR, B, PAIR), bf16),
            pltpu.VMEM((slots, length), f32),
            pltpu.VMEM((cols, length), bf16),
            pltpu.VMEM((cols, length), bf16),
            pltpu.VMEM((2 * cols, length), bf16),
            pltpu.VMEM((cols, length), f32),
            pltpu.VMEM((rows, cols, PAIR), bf16),
            pltpu.VMEM((slots, cols, PAIR), f32),
            pltpu.VMEM((slots + 1, cols, PAIR), f32),
            pltpu.VMEM((3, n_row, cols, 2 * PAIR), bf16),
            pltpu.VMEM((3, n_row, cols, 2 * PAIR), bf16),
            pltpu.VMEM((n_col, cols, length), bf16),
            pltpu.VMEM((n_row, piece, total_cols), sum_type),
            pltpu.VMEM((n_row, piece, total_cols), sum_type),
            pltpu.VMEM((piece, total_cols), sum_type),
            dma((tiles,)),
            dma((3, n_row)), dma((3, n_row)),
            dma((n_col,)), dma((n_col,)),
            dma((n_row,)), dma((n_row,)),
            dma((n_row,)), dma((n_row,)),
        ],
        compiler_params=pltpu.CompilerParams(
            collective_id=0, has_side_effects=True, vmem_limit_bytes=56 * 1024 * 1024
        ),
    )(send_rows, by_slot, holder, vectors, diagonal, upper)

    filtered, gram, projected = pl.pallas_call(
        functools.partial(output_kernel, cols),
        out_shape=(
            jax.ShapeDtypeStruct((cols, length), bf16),
            jax.ShapeDtypeStruct((cols, total_cols), f32),
            jax.ShapeDtypeStruct((cols, total_cols), f32),
        ),
        in_specs=[vmem, vmem],
        out_specs=(vmem, vmem, vmem),
    )(ordered, sums)
    return filtered, gram.T, projected.T


def solution(mesh):
    return jax.shard_map(
        on_device,
        mesh=mesh,
        in_specs=(P("col", "row"), P("row", None, None), P("row"), P("row", None), P("row")),
        out_specs=(P("col", "row"), P(None, "col"), P(None, "col")),
        check_vma=False,
    )
```

```python
import functools

import jax
import jax.numpy as jnp
from jax import lax
from jax.experimental import pallas as pl
from jax.experimental.pallas import tpu as pltpu
from jax.sharding import PartitionSpec as P

B = 64
K = 12
PAIR = 2 * B
TILE = 256
UNROLL = 8
ROWS_STEP = 16
HALF = B // 2

center_value = 0.25
half_width = 1.5

MESH = pl.DeviceIdType.MESH
NN = (((1,), (0,)), ((), ()))
NT = (((1,), (1,)), ((), ()))


def dot(a, b, dims):
    return lax.dot_general(a, b, dims, preferred_element_type=jnp.float32)


def order_matrix():
    row_at = lax.broadcasted_iota(jnp.int32, (TILE, TILE), 0)
    col_at = lax.broadcasted_iota(jnp.int32, (TILE, TILE), 1)
    within = row_at & (B - 1)
    target = (row_at - within) + (within & 1) * HALF + ((within >> 1) & 1) * (HALF // 2) + (within >> 2)
    return jnp.where(target == col_at, 1.0, 0.0).astype(jnp.bfloat16)


def build_kernel(rows, sources, counts, h, upper, diagonal, holder, order, swap, marks, placed, remote):
    step = pl.program_id(0)
    here = upper.shape[0]
    slots = remote.shape[0] - 1
    pieces = B * B // TILE
    first_row = step * here
    bf16 = jnp.bfloat16

    @pl.when(step == 0)
    def _():
        order[...] = order_matrix()
        row_at = lax.broadcasted_iota(jnp.int32, (TILE, TILE), 0)
        col_at = lax.broadcasted_iota(jnp.int32, (TILE, TILE), 1)
        swap[...] = jnp.where(col_at == (row_at & (pieces - 1)) * here + (row_at >> 4), 1.0, 0.0).astype(bf16)
        side = lax.broadcasted_iota(jnp.int32, (here, PAIR), 1) >> 6
        for wanted in range(3):
            marks[wanted] = jnp.where(side == wanted, 1.0, 0.0).astype(bf16)

    def clear_body(row, carry):
        upper[row] = jnp.zeros_like(upper[row])
        return carry

    lax.fori_loop(0, here, clear_body, 0)

    def order_body(pack, carry):
        for inner in range(2):
            slot = 2 * pack + inner
            lanes = jnp.concatenate([h[slot, :, at * TILE : (at + 1) * TILE] for at in range(pieces)], 0)
            swapped = dot(swap[...], lanes, NN).astype(bf16)
            value = dot(swapped, order[...], NN)
            for part in range(2):
                straight = value[:, part * PAIR : (part + 1) * PAIR]
                turned = pltpu.roll(straight, B, 1)
                placed[slot, 0, part] = straight.astype(bf16).reshape(here, pieces, PAIR)
                placed[slot, 1, part] = turned.astype(bf16).reshape(here, pieces, PAIR)
        return carry

    lax.fori_loop(0, K // 2, order_body, 0)

    def marked(slot, row, half, wanted):
        mark = marks[wanted]
        return jnp.concatenate(
            [placed[slot, turned, part, row] * mark for turned in (half, 1 - half) for part in range(2)], 0
        )

    def add_body(slot, carry):
        for group in range(here // UNROLL):
            news = []
            for row in range(group * UNROLL, (group + 1) * UNROLL):
                source = sources[slot, first_row + row]
                half = source & 1
                local = source < rows
                used = jnp.logical_and(slot < counts[first_row + row], local)
                pair = jnp.where(local, source >> 1, 0)
                new = upper[row, pair] + marked(slot, row, half, jnp.where(used, half, 2))
                news.append((row, pair, new))
            for row, pair, new in news:
                upper[row, pair] = new
        return carry

    lax.fori_loop(0, K, add_body, 0)

    def remote_body(group, carry):
        news = []
        for inner in range(4):
            row = 4 * group + inner
            for slot in (1, 2):
                source = sources[slot, first_row + row]
                at = jnp.where(source >= rows, source - rows, slots)
                holder[at] = first_row + row
                half = source & 1
                news.append((at, marked(slot, row, half, half)))
        for at, new in news:
            remote[at] = new
        return carry

    lax.fori_loop(0, here // 4, remote_body, 0)

    @pl.when(step == pl.num_programs(0) - 1)
    def _():
        diagonal[...] = jnp.zeros_like(diagonal)
        for slot in range(slots):
            part = slot % 4
            diagonal[slot // 4, pl.ds(part * B, B), pl.ds((part // 2) * PAIR, PAIR)] = remote[slot]


def output_kernel(cols, ordered, sums, filtered, gram, projected):
    order = order_matrix()
    for tile in range(ordered.shape[1] // TILE):
        here = pl.ds(tile * TILE, TILE)
        filtered[:, here] = dot(ordered[:, here], order, NT).astype(jnp.bfloat16)
    count, piece = sums.shape[0], sums.shape[1]
    for at in range(count):
        value = sums[at].astype(jnp.float32)
        first = at * piece
        if first < cols:
            gram[pl.ds(first, piece), :] = value
        else:
            projected[pl.ds(first - cols, piece), :] = value


def filter_kernel(
    n_row, n_col, send_rows, sources, holder, x_in, diagonal, dense_in,
    filtered, sum_in,
    dense, mask,
    x0, step_one, stacked, total, blocks, spread, upspread, out_buf, in_buf, gathered,
    piece_out, piece_in, sum_out,
    dense_sem,
    send_sem, recv_sem, col_send, col_recv, piece_send, piece_recv, sum_send, sum_recv,
):
    me = lax.axis_index("row")
    mine = lax.axis_index("col")
    cols, length = x_in.shape
    rows = length // B
    pairs = length // PAIR
    slots = 2 * n_row
    tiles = length // TILE
    per_tile = TILE // B
    bf16 = jnp.bfloat16
    f32 = jnp.float32

    barrier = pltpu.get_barrier_semaphore()
    for step in range(1, n_row):
        pl.semaphore_signal(barrier, inc=1, device_id={"row": lax.rem(me + step, n_row)}, device_id_type=MESH)
    for step in range(1, n_col):
        pl.semaphore_signal(barrier, inc=1, device_id={"col": lax.rem(mine + step, n_col)}, device_id_type=MESH)

    def dense_copy(tile):
        here = pl.ds(tile * per_tile, per_tile)
        return pltpu.make_async_copy(
            dense_in.at[here], dense.at[here], dense_sem.at[tile]
        )

    for tile in range(tiles):
        dense_copy(tile).start()

    def columns(at, width):
        return pl.ds(pl.multiple_of(at * width, width), width)

    low = lax.broadcasted_iota(jnp.int32, (cols, PAIR), 1) < B

    def both(values):
        turned = pltpu.roll(values, B, 1)
        return jnp.where(low, values, turned), jnp.where(low, turned, values)

    lane_block = lax.broadcasted_iota(jnp.int32, (1, length), 1) >> 6

    def mask_body(slot, carry):
        mask[pl.ds(slot, 1), :] = jnp.where(lane_block == send_rows[slot], 1.0, 0.0)
        return carry

    lax.fori_loop(0, slots, mask_body, 0)

    def keep_blocks(pair, values):
        first, second = both(values)
        blocks[2 * pair] = first.astype(bf16)
        blocks[2 * pair + 1] = second.astype(bf16)

    order = order_matrix()
    for tile in range(tiles):
        here = pl.ds(tile * TILE, TILE)
        value = dot(x_in[:, here], order, NN)
        x0[:, here] = value.astype(bf16)
        keep_blocks(2 * tile, value[:, :PAIR])
        keep_blocks(2 * tile + 1, value[:, PAIR:])

    upspread[slots] = jnp.zeros((cols, PAIR), f32)

    def arrived_at(row, slot):
        source = sources[slot, row]
        return upspread[jnp.where(source >= rows, source - rows, slots)]

    pl.semaphore_wait(barrier, n_row + n_col - 2)

    def row_copy(phase, slot_here, slot_there, peer):
        return pltpu.make_async_remote_copy(
            src_ref=out_buf.at[phase, slot_here],
            dst_ref=in_buf.at[phase, slot_there],
            send_sem=send_sem.at[phase, slot_here],
            recv_sem=recv_sem.at[phase, slot_there],
            device_id={"row": peer},
            device_id_type=MESH,
        )

    def pick(first, second):
        return jnp.where(low, blocks[first].astype(f32), blocks[second].astype(f32)).astype(bf16)

    def apply_operator(phase, source, finish, beside=None):
        for pack in range(slots // 4):
            at = 4 * pack
            near = jnp.concatenate([pick(holder[at], holder[at + 1]), pick(holder[at + 2], holder[at + 3])], 1)
            product = dot(near, diagonal[pack], NN).astype(bf16)
            for inner in range(2):
                peer = 2 * pack + inner
                out_buf[phase, peer, :, pl.ds(0, PAIR)] = pick(send_rows[2 * peer], send_rows[2 * peer + 1])
                out_buf[phase, peer, :, pl.ds(PAIR, PAIR)] = product[:, inner * PAIR : (inner + 1) * PAIR]
        for step in range(1, n_row):
            peer = lax.rem(me + step, n_row)
            row_copy(phase, peer, me, peer).start()
        in_buf[phase, me] = out_buf[phase, me]

        def local_body(tile, carry):
            down = jnp.concatenate([dense[:, 2 * tile + side].reshape(length, PAIR) for side in range(2)], 1)
            along = jnp.concatenate(
                [dense[pl.ds(tile * per_tile, per_tile), pair].reshape(TILE, PAIR) for pair in range(pairs)], 1
            )
            total[:, columns(tile, TILE)] = dot(source[...], down, NN) + dot(source[...], along, NT)
            return carry

        if phase == 0:
            for tile in range(tiles):
                dense_copy(tile).wait()

        lax.fori_loop(0, tiles, local_body, 0)
        for step in range(1, n_row):
            peer = lax.rem(me + step, n_row)
            row_copy(phase, peer, peer, peer).wait_recv()
        if beside is not None:
            beside()

        for pack in range(slots // 4):
            far = jnp.concatenate([in_buf[phase, 2 * pack + inner, :, pl.ds(0, PAIR)] for inner in range(2)], 1)
            product = dot(far, diagonal[pack], NT)
            for inner in range(2):
                peer = 2 * pack + inner
                first, second = both(product[:, inner * PAIR : (inner + 1) * PAIR])
                upspread[2 * peer] = first
                upspread[2 * peer + 1] = second
                first, second = both(in_buf[phase, peer, :, pl.ds(PAIR, PAIR)].astype(f32))
                spread[2 * peer] = first
                spread[2 * peer + 1] = second

        def finish_body(pair, carry):
            here = columns(pair, PAIR)
            value = total[:, here] + jnp.where(
                low,
                arrived_at(2 * pair, 1) + arrived_at(2 * pair, 2),
                arrived_at(2 * pair + 1, 1) + arrived_at(2 * pair + 1, 2),
            )
            for slot in range(slots):
                value = value + spread[slot] * mask[pl.ds(slot, 1), here]
            finish(pair, here, value)
            return carry

        lax.fori_loop(0, pairs, finish_body, 0)

    def first_finish(pair, here, value):
        new = ((value - center_value * x0[:, here].astype(f32)) / half_width).astype(bf16)
        step_one[:, here] = new
        keep_blocks(pair, new.astype(f32))

    def second_finish(pair, here, value):
        old = step_one[:, here].astype(f32)
        new = (2.0 * (value - center_value * old) / half_width - x0[:, here].astype(f32)).astype(bf16)
        stacked[pl.ds(0, cols), here] = new
        gathered[mine, :, here] = new
        filtered[:, here] = new
        keep_blocks(pair, new.astype(f32))

    def third_finish(pair, here, value):
        stacked[pl.ds(cols, cols), here] = value.astype(bf16)

    def col_copy(slot_here, slot_there, sem_at, peer):
        return pltpu.make_async_remote_copy(
            src_ref=gathered.at[slot_here],
            dst_ref=gathered.at[slot_there],
            send_sem=col_send.at[sem_at],
            recv_sem=col_recv.at[slot_there],
            device_id={"col": peer},
            device_id_type=MESH,
        )

    sibling = mine + 1 - 2 * lax.rem(mine, 2)
    across = [lax.rem(mine + 2 * step, n_col) for step in range(1, n_col // 2)]

    def start_gather():
        for at, peer in enumerate(across):
            col_copy(mine, mine, at, peer).start()
        col_copy(mine, mine, len(across), sibling).start()

    def forward_gather():
        for at, peer in enumerate(across):
            col_copy(peer, peer, at, peer).wait_recv()
            col_copy(peer, peer, len(across) + 1 + at, sibling).start()

    def end_gather():
        col_copy(sibling, sibling, 0, sibling).wait_recv()
        for peer in across:
            other = peer + 1 - 2 * lax.rem(peer, 2)
            col_copy(other, other, 0, sibling).wait_recv()

    apply_operator(0, x0, first_finish)
    apply_operator(1, step_one, second_finish)
    start_gather()
    apply_operator(2, stacked.at[pl.ds(0, cols)], third_finish, forward_gather)
    end_gather()

    piece = 2 * cols // n_row
    part = dot(stacked[...], gathered[...].reshape(n_col * cols, length), NT)
    for at in range(n_row):
        piece_out[at] = part[at * piece : (at + 1) * piece].astype(piece_out.dtype)

    def piece_copy(slot_here, slot_there, peer):
        return pltpu.make_async_remote_copy(
            src_ref=piece_out.at[slot_here],
            dst_ref=piece_in.at[slot_there],
            send_sem=piece_send.at[slot_here],
            recv_sem=piece_recv.at[slot_there],
            device_id={"row": peer},
            device_id_type=MESH,
        )

    def sum_copy(slot_there, peer):
        return pltpu.make_async_remote_copy(
            src_ref=sum_out,
            dst_ref=sum_in.at[slot_there],
            send_sem=sum_send.at[peer],
            recv_sem=sum_recv.at[slot_there],
            device_id={"row": peer},
            device_id_type=MESH,
        )

    peers = [lax.rem(me + step, n_row) for step in range(1, n_row)]
    for peer in peers:
        piece_copy(peer, me, peer).start()
    piece_in[me] = piece_out[me]
    for peer in peers:
        piece_copy(peer, peer, peer).wait_recv()
    summed = piece_in[0].astype(f32)
    for peer in range(1, n_row):
        summed = summed + piece_in[peer].astype(f32)
    sum_out[...] = summed.astype(sum_out.dtype)
    for peer in peers:
        sum_copy(me, peer).start()
    sum_in[me] = sum_out[...]
    for peer in peers:
        sum_copy(peer, peer).wait_recv()
    for peer in peers:
        for phase in range(3):
            row_copy(phase, peer, me, peer).wait_send()
        piece_copy(peer, me, peer).wait_send()
        sum_copy(me, peer).wait_send()
    for at, peer in enumerate(across):
        col_copy(mine, mine, at, peer).wait_send()
        col_copy(peer, peer, len(across) + 1 + at, sibling).wait_send()
    col_copy(mine, mine, len(across), sibling).wait_send()


def on_device(vectors, hblocks, counts, sources, send_rows):
    rows = hblocks.shape[0]
    cols, length = vectors.shape
    slots = send_rows.shape[0]
    n_row = lax.axis_size("row")
    n_col = lax.axis_size("col")
    assert slots == 2 * n_row
    tiles = length // TILE
    total_cols = n_col * cols
    piece = 2 * cols // n_row
    sum_type = jnp.bfloat16 if piece % 16 == 0 else jnp.float32
    smem = pl.BlockSpec(memory_space=pltpu.SMEM)
    vmem = pl.BlockSpec(memory_space=pltpu.VMEM)
    dma = pltpu.SemaphoreType.DMA
    bf16 = jnp.bfloat16
    f32 = jnp.float32
    by_slot = sources.T
    upper, diagonal, holder = pl.pallas_call(
        functools.partial(build_kernel, rows),
        grid=(rows // ROWS_STEP,),
        out_shape=(
            jax.ShapeDtypeStruct((rows, rows // 2, B, PAIR), bf16),
            jax.ShapeDtypeStruct((slots // 4, TILE, TILE), bf16),
            jax.ShapeDtypeStruct((slots + 1,), jnp.int32),
        ),
        in_specs=[smem, smem, pl.BlockSpec((K, ROWS_STEP, B * B), lambda step: (0, step, 0))],
        out_specs=(
            pl.BlockSpec((ROWS_STEP, rows // 2, B, PAIR), lambda step: (step, 0, 0, 0)),
            pl.BlockSpec((slots // 4, TILE, TILE), lambda step: (0, 0, 0)),
            smem,
        ),
        scratch_shapes=[
            pltpu.VMEM((TILE, TILE), bf16),
            pltpu.VMEM((TILE, TILE), bf16),
            pltpu.VMEM((3, ROWS_STEP, PAIR), bf16),
            pltpu.VMEM((K, 2, 2, ROWS_STEP, B * B // TILE, PAIR), bf16),
            pltpu.VMEM((slots + 1, B, PAIR), bf16),
        ],
        compiler_params=pltpu.CompilerParams(vmem_limit_bytes=56 * 1024 * 1024),
    )(by_slot, counts, hblocks.transpose(1, 0, 2))

    ordered, sums = pl.pallas_call(
        functools.partial(filter_kernel, n_row, n_col),
        out_shape=(
            jax.ShapeDtypeStruct((cols, length), bf16),
            jax.ShapeDtypeStruct((n_row, piece, total_cols), sum_type),
        ),
        in_specs=[smem, smem, smem, vmem, vmem, pl.BlockSpec(memory_space=pl.ANY)],
        out_specs=(vmem, vmem),
        scratch_shapes=[
            pltpu.VMEM((rows, length // PAIR, B, PAIR), bf16),
            pltpu.VMEM((slots, length), f32),
            pltpu.VMEM((cols, length), bf16),
            pltpu.VMEM((cols, length), bf16),
            pltpu.VMEM((2 * cols, length), bf16),
            pltpu.VMEM((cols, length), f32),
            pltpu.VMEM((rows, cols, PAIR), bf16),
            pltpu.VMEM((slots, cols, PAIR), f32),
            pltpu.VMEM((slots + 1, cols, PAIR), f32),
            pltpu.VMEM((3, n_row, cols, 2 * PAIR), bf16),
            pltpu.VMEM((3, n_row, cols, 2 * PAIR), bf16),
            pltpu.VMEM((n_col, cols, length), bf16),
            pltpu.VMEM((n_row, piece, total_cols), sum_type),
            pltpu.VMEM((n_row, piece, total_cols), sum_type),
            pltpu.VMEM((piece, total_cols), sum_type),
            dma((tiles,)),
            dma((3, n_row)), dma((3, n_row)),
            dma((n_col,)), dma((n_col,)),
            dma((n_row,)), dma((n_row,)),
            dma((n_row,)), dma((n_row,)),
        ],
        compiler_params=pltpu.CompilerParams(
            collective_id=0, has_side_effects=True, vmem_limit_bytes=56 * 1024 * 1024
        ),
    )(send_rows, by_slot, holder, vectors, diagonal, upper)

    filtered, gram, projected = pl.pallas_call(
        functools.partial(output_kernel, cols),
        out_shape=(
            jax.ShapeDtypeStruct((cols, length), bf16),
            jax.ShapeDtypeStruct((cols, total_cols), f32),
            jax.ShapeDtypeStruct((cols, total_cols), f32),
        ),
        in_specs=[vmem, vmem],
        out_specs=(vmem, vmem, vmem),
    )(ordered, sums)
    return filtered, gram.T, projected.T


def solution(mesh):
    return jax.shard_map(
        on_device,
        mesh=mesh,
        in_specs=(P("col", "row"), P("row", None, None), P("row"), P("row", None), P("row")),
        out_specs=(P("col", "row"), P(None, "col"), P(None, "col")),
        check_vma=False,
    )
```

```python
import functools

import jax
import jax.numpy as jnp
from jax import lax
from jax.experimental import pallas as pl
from jax.experimental.pallas import tpu as pltpu
from jax.sharding import PartitionSpec as P

B = 64
K = 12
PAIR = 2 * B
TILE = 256
UNROLL = 8
ROWS_STEP = 16
HALF = B // 2

center_value = 0.25
half_width = 1.5

MESH = pl.DeviceIdType.MESH
NN = (((1,), (0,)), ((), ()))
NT = (((1,), (1,)), ((), ()))


def dot(a, b, dims):
    return lax.dot_general(a, b, dims, preferred_element_type=jnp.float32)


def order_matrix():
    row_at = lax.broadcasted_iota(jnp.int32, (TILE, TILE), 0)
    col_at = lax.broadcasted_iota(jnp.int32, (TILE, TILE), 1)
    within = row_at & (B - 1)
    target = (row_at - within) + (within & 1) * HALF + ((within >> 1) & 1) * (HALF // 2) + (within >> 2)
    return jnp.where(target == col_at, 1.0, 0.0).astype(jnp.bfloat16)


def build_kernel(rows, sources, counts, h, upper, diagonal, holder, order, swap, marks, placed, remote):
    step = pl.program_id(0)
    here = upper.shape[0]
    slots = remote.shape[0] - 1
    pieces = B * B // TILE
    first_row = step * here
    bf16 = jnp.bfloat16

    @pl.when(step == 0)
    def _():
        order[...] = order_matrix()
        row_at = lax.broadcasted_iota(jnp.int32, (TILE, TILE), 0)
        col_at = lax.broadcasted_iota(jnp.int32, (TILE, TILE), 1)
        swap[...] = jnp.where(col_at == (row_at & (pieces - 1)) * here + (row_at >> 4), 1.0, 0.0).astype(bf16)
        side = lax.broadcasted_iota(jnp.int32, (here, PAIR), 1) >> 6
        for wanted in range(3):
            marks[wanted] = jnp.where(side == wanted, 1.0, 0.0).astype(bf16)

    def clear_body(row, carry):
        upper[row] = jnp.zeros_like(upper[row])
        return carry

    lax.fori_loop(0, here, clear_body, 0)

    def order_body(pack, carry):
        for inner in range(2):
            slot = 2 * pack + inner
            lanes = jnp.concatenate([h[slot, :, at * TILE : (at + 1) * TILE] for at in range(pieces)], 0)
            swapped = dot(swap[...], lanes, NN).astype(bf16)
            value = dot(swapped, order[...], NN)
            for part in range(2):
                straight = value[:, part * PAIR : (part + 1) * PAIR]
                turned = pltpu.roll(straight, B, 1)
                placed[slot, 0, part] = straight.astype(bf16).reshape(here, pieces, PAIR)
                placed[slot, 1, part] = turned.astype(bf16).reshape(here, pieces, PAIR)
        return carry

    lax.fori_loop(0, K // 2, order_body, 0)

    def marked(slot, row, half, wanted):
        mark = marks[wanted]
        return jnp.concatenate(
            [placed[slot, turned, part, row] * mark for turned in (half, 1 - half) for part in range(2)], 0
        )

    def add_body(slot, carry):
        for group in range(here // UNROLL):
            news = []
            for row in range(group * UNROLL, (group + 1) * UNROLL):
                source = sources[slot, first_row + row]
                half = source & 1
                local = source < rows
                used = jnp.logical_and(slot < counts[first_row + row], local)
                pair = jnp.where(local, source >> 1, 0)
                new = upper[row, pair] + marked(slot, row, half, jnp.where(used, half, 2))
                news.append((row, pair, new))
            for row, pair, new in news:
                upper[row, pair] = new
        return carry

    lax.fori_loop(0, K, add_body, 0)

    def remote_body(group, carry):
        news = []
        for inner in range(4):
            row = 4 * group + inner
            for slot in (1, 2):
                source = sources[slot, first_row + row]
                at = jnp.where(source >= rows, source - rows, slots)
                holder[at] = first_row + row
                half = source & 1
                news.append((at, marked(slot, row, half, half)))
        for at, new in news:
            remote[at] = new
        return carry

    lax.fori_loop(0, here // 4, remote_body, 0)

    @pl.when(step == pl.num_programs(0) - 1)
    def _():
        diagonal[...] = jnp.zeros_like(diagonal)
        for slot in range(slots):
            part = slot % 4
            diagonal[slot // 4, pl.ds(part * B, B), pl.ds((part // 2) * PAIR, PAIR)] = remote[slot]


def output_kernel(cols, ordered, sums, filtered, gram, projected):
    order = order_matrix()
    for tile in range(ordered.shape[1] // TILE):
        here = pl.ds(tile * TILE, TILE)
        filtered[:, here] = dot(ordered[:, here], order, NT).astype(jnp.bfloat16)
    count, piece = sums.shape[0], sums.shape[1]
    for at in range(count):
        value = sums[at].astype(jnp.float32)
        first = at * piece
        if first < cols:
            gram[pl.ds(first, piece), :] = value
        else:
            projected[pl.ds(first - cols, piece), :] = value


def filter_kernel(
    n_row, n_col, send_rows, sources, holder, x_in, diagonal, dense_in,
    filtered, sum_in,
    dense, mask,
    x0, step_one, stacked, total, blocks, spread, upspread, out_buf, in_buf, gathered,
    piece_out, piece_in, sum_out,
    dense_sem,
    send_sem, recv_sem, col_send, col_recv, piece_send, piece_recv, sum_send, sum_recv,
):
    me = lax.axis_index("row")
    mine = lax.axis_index("col")
    cols, length = x_in.shape
    rows = length // B
    pairs = length // PAIR
    slots = 2 * n_row
    tiles = length // TILE
    per_tile = TILE // B
    bf16 = jnp.bfloat16
    f32 = jnp.float32

    barrier = pltpu.get_barrier_semaphore()
    for step in range(1, n_row):
        pl.semaphore_signal(barrier, inc=1, device_id={"row": lax.rem(me + step, n_row)}, device_id_type=MESH)
    for step in range(1, n_col):
        pl.semaphore_signal(barrier, inc=1, device_id={"col": lax.rem(mine + step, n_col)}, device_id_type=MESH)

    def dense_copy(tile):
        here = pl.ds(tile * per_tile, per_tile)
        return pltpu.make_async_copy(
            dense_in.at[here], dense.at[here], dense_sem.at[tile]
        )

    for tile in range(tiles):
        dense_copy(tile).start()

    def columns(at, width):
        return pl.ds(pl.multiple_of(at * width, width), width)

    low = lax.broadcasted_iota(jnp.int32, (cols, PAIR), 1) < B

    def both(values):
        turned = pltpu.roll(values, B, 1)
        return jnp.where(low, values, turned), jnp.where(low, turned, values)

    lane_block = lax.broadcasted_iota(jnp.int32, (1, length), 1) >> 6

    def mask_body(slot, carry):
        mask[pl.ds(slot, 1), :] = jnp.where(lane_block == send_rows[slot], 1.0, 0.0)
        return carry

    lax.fori_loop(0, slots, mask_body, 0)

    def keep_blocks(pair, values):
        first, second = both(values)
        blocks[2 * pair] = first.astype(bf16)
        blocks[2 * pair + 1] = second.astype(bf16)

    order = order_matrix()
    for tile in range(tiles):
        here = pl.ds(tile * TILE, TILE)
        value = dot(x_in[:, here], order, NN)
        x0[:, here] = value.astype(bf16)
        keep_blocks(2 * tile, value[:, :PAIR])
        keep_blocks(2 * tile + 1, value[:, PAIR:])

    upspread[slots] = jnp.zeros((cols, PAIR), f32)

    def arrived_at(row, slot):
        source = sources[slot, row]
        return upspread[jnp.where(source >= rows, source - rows, slots)]

    pl.semaphore_wait(barrier, n_row + n_col - 2)

    def row_copy(phase, kind, slot_here, slot_there, peer):
        return pltpu.make_async_remote_copy(
            src_ref=out_buf.at[phase, kind, slot_here],
            dst_ref=in_buf.at[phase, kind, slot_there],
            send_sem=send_sem.at[phase, kind, slot_here],
            recv_sem=recv_sem.at[phase, kind, slot_there],
            device_id={"row": peer},
            device_id_type=MESH,
        )

    def send_all(phase, kind):
        for step in range(1, n_row):
            peer = lax.rem(me + step, n_row)
            row_copy(phase, kind, peer, me, peer).start()
        in_buf[phase, kind, me] = out_buf[phase, kind, me]

    def wait_all(phase, kind):
        for step in range(1, n_row):
            peer = lax.rem(me + step, n_row)
            row_copy(phase, kind, peer, peer, peer).wait_recv()

    def pick(first, second):
        return jnp.where(low, blocks[first].astype(f32), blocks[second].astype(f32)).astype(bf16)

    def apply_operator(phase, source, finish, beside=None):
        for peer in range(n_row):
            out_buf[phase, 0, peer] = pick(send_rows[2 * peer], send_rows[2 * peer + 1])
        send_all(phase, 0)
        for pack in range(slots // 4):
            at = 4 * pack
            near = jnp.concatenate([pick(holder[at], holder[at + 1]), pick(holder[at + 2], holder[at + 3])], 1)
            product = dot(near, diagonal[pack], NN).astype(bf16)
            for inner in range(2):
                out_buf[phase, 1, 2 * pack + inner] = product[:, inner * PAIR : (inner + 1) * PAIR]
        send_all(phase, 1)

        def local_body(tile, carry):
            down = jnp.concatenate([dense[:, 2 * tile + side].reshape(length, PAIR) for side in range(2)], 1)
            along = jnp.concatenate(
                [dense[pl.ds(tile * per_tile, per_tile), pair].reshape(TILE, PAIR) for pair in range(pairs)], 1
            )
            total[:, columns(tile, TILE)] = dot(source[...], down, NN) + dot(source[...], along, NT)
            return carry

        if phase == 0:
            for tile in range(tiles):
                dense_copy(tile).wait()

        lax.fori_loop(0, tiles, local_body, 0)
        wait_all(phase, 0)
        for pack in range(slots // 4):
            far = jnp.concatenate([in_buf[phase, 0, 2 * pack + inner] for inner in range(2)], 1)
            product = dot(far, diagonal[pack], NT)
            for inner in range(2):
                peer = 2 * pack + inner
                first, second = both(product[:, inner * PAIR : (inner + 1) * PAIR])
                upspread[2 * peer] = first
                upspread[2 * peer + 1] = second
        wait_all(phase, 1)
        for peer in range(n_row):
            first, second = both(in_buf[phase, 1, peer].astype(f32))
            spread[2 * peer] = first
            spread[2 * peer + 1] = second
        if beside is not None:
            beside()

        def finish_body(pair, carry):
            here = columns(pair, PAIR)
            value = total[:, here] + jnp.where(
                low,
                arrived_at(2 * pair, 1) + arrived_at(2 * pair, 2),
                arrived_at(2 * pair + 1, 1) + arrived_at(2 * pair + 1, 2),
            )
            for slot in range(slots):
                value = value + spread[slot] * mask[pl.ds(slot, 1), here]
            finish(pair, here, value)
            return carry

        lax.fori_loop(0, pairs, finish_body, 0)

    def first_finish(pair, here, value):
        new = ((value - center_value * x0[:, here].astype(f32)) / half_width).astype(bf16)
        step_one[:, here] = new
        keep_blocks(pair, new.astype(f32))

    def second_finish(pair, here, value):
        old = step_one[:, here].astype(f32)
        new = (2.0 * (value - center_value * old) / half_width - x0[:, here].astype(f32)).astype(bf16)
        stacked[pl.ds(0, cols), here] = new
        gathered[mine, :, here] = new
        filtered[:, here] = new
        keep_blocks(pair, new.astype(f32))

    def third_finish(pair, here, value):
        stacked[pl.ds(cols, cols), here] = value.astype(bf16)

    def col_copy(slot_here, slot_there, sem_at, peer):
        return pltpu.make_async_remote_copy(
            src_ref=gathered.at[slot_here],
            dst_ref=gathered.at[slot_there],
            send_sem=col_send.at[sem_at],
            recv_sem=col_recv.at[slot_there],
            device_id={"col": peer},
            device_id_type=MESH,
        )

    sibling = mine + 1 - 2 * lax.rem(mine, 2)
    across = [lax.rem(mine + 2 * step, n_col) for step in range(1, n_col // 2)]

    def start_gather():
        for at, peer in enumerate(across):
            col_copy(mine, mine, at, peer).start()
        col_copy(mine, mine, len(across), sibling).start()

    def forward_gather():
        for at, peer in enumerate(across):
            col_copy(peer, peer, at, peer).wait_recv()
            col_copy(peer, peer, len(across) + 1 + at, sibling).start()

    def end_gather():
        col_copy(sibling, sibling, 0, sibling).wait_recv()
        for peer in across:
            other = peer + 1 - 2 * lax.rem(peer, 2)
            col_copy(other, other, 0, sibling).wait_recv()

    apply_operator(0, x0, first_finish)
    apply_operator(1, step_one, second_finish)
    start_gather()
    apply_operator(2, stacked.at[pl.ds(0, cols)], third_finish, forward_gather)
    end_gather()

    piece = 2 * cols // n_row
    part = dot(stacked[...], gathered[...].reshape(n_col * cols, length), NT)
    for at in range(n_row):
        piece_out[at] = part[at * piece : (at + 1) * piece].astype(piece_out.dtype)

    def piece_copy(slot_here, slot_there, peer):
        return pltpu.make_async_remote_copy(
            src_ref=piece_out.at[slot_here],
            dst_ref=piece_in.at[slot_there],
            send_sem=piece_send.at[slot_here],
            recv_sem=piece_recv.at[slot_there],
            device_id={"row": peer},
            device_id_type=MESH,
        )

    def sum_copy(slot_there, peer):
        return pltpu.make_async_remote_copy(
            src_ref=sum_out,
            dst_ref=sum_in.at[slot_there],
            send_sem=sum_send.at[peer],
            recv_sem=sum_recv.at[slot_there],
            device_id={"row": peer},
            device_id_type=MESH,
        )

    peers = [lax.rem(me + step, n_row) for step in range(1, n_row)]
    for peer in peers:
        piece_copy(peer, me, peer).start()
    piece_in[me] = piece_out[me]
    for peer in peers:
        piece_copy(peer, peer, peer).wait_recv()
    summed = piece_in[0].astype(f32)
    for peer in range(1, n_row):
        summed = summed + piece_in[peer].astype(f32)
    sum_out[...] = summed.astype(sum_out.dtype)
    for peer in peers:
        sum_copy(me, peer).start()
    sum_in[me] = sum_out[...]
    for peer in peers:
        sum_copy(peer, peer).wait_recv()
    for peer in peers:
        for phase in range(3):
            row_copy(phase, 0, peer, me, peer).wait_send()
            row_copy(phase, 1, peer, me, peer).wait_send()
        piece_copy(peer, me, peer).wait_send()
        sum_copy(me, peer).wait_send()
    for at, peer in enumerate(across):
        col_copy(mine, mine, at, peer).wait_send()
        col_copy(peer, peer, len(across) + 1 + at, sibling).wait_send()
    col_copy(mine, mine, len(across), sibling).wait_send()


def on_device(vectors, hblocks, counts, sources, send_rows):
    rows = hblocks.shape[0]
    cols, length = vectors.shape
    slots = send_rows.shape[0]
    n_row = lax.axis_size("row")
    n_col = lax.axis_size("col")
    assert slots == 2 * n_row
    tiles = length // TILE
    total_cols = n_col * cols
    piece = 2 * cols // n_row
    sum_type = jnp.bfloat16 if piece % 16 == 0 else jnp.float32
    smem = pl.BlockSpec(memory_space=pltpu.SMEM)
    vmem = pl.BlockSpec(memory_space=pltpu.VMEM)
    dma = pltpu.SemaphoreType.DMA
    bf16 = jnp.bfloat16
    f32 = jnp.float32
    by_slot = sources.T
    upper, diagonal, holder = pl.pallas_call(
        functools.partial(build_kernel, rows),
        grid=(rows // ROWS_STEP,),
        out_shape=(
            jax.ShapeDtypeStruct((rows, rows // 2, B, PAIR), bf16),
            jax.ShapeDtypeStruct((slots // 4, TILE, TILE), bf16),
            jax.ShapeDtypeStruct((slots + 1,), jnp.int32),
        ),
        in_specs=[smem, smem, pl.BlockSpec((K, ROWS_STEP, B * B), lambda step: (0, step, 0))],
        out_specs=(
            pl.BlockSpec((ROWS_STEP, rows // 2, B, PAIR), lambda step: (step, 0, 0, 0)),
            pl.BlockSpec((slots // 4, TILE, TILE), lambda step: (0, 0, 0)),
            smem,
        ),
        scratch_shapes=[
            pltpu.VMEM((TILE, TILE), bf16),
            pltpu.VMEM((TILE, TILE), bf16),
            pltpu.VMEM((3, ROWS_STEP, PAIR), bf16),
            pltpu.VMEM((K, 2, 2, ROWS_STEP, B * B // TILE, PAIR), bf16),
            pltpu.VMEM((slots + 1, B, PAIR), bf16),
        ],
        compiler_params=pltpu.CompilerParams(vmem_limit_bytes=56 * 1024 * 1024),
    )(by_slot, counts, hblocks.transpose(1, 0, 2))

    ordered, sums = pl.pallas_call(
        functools.partial(filter_kernel, n_row, n_col),
        out_shape=(
            jax.ShapeDtypeStruct((cols, length), bf16),
            jax.ShapeDtypeStruct((n_row, piece, total_cols), sum_type),
        ),
        in_specs=[smem, smem, smem, vmem, vmem, pl.BlockSpec(memory_space=pl.ANY)],
        out_specs=(vmem, vmem),
        scratch_shapes=[
            pltpu.VMEM((rows, length // PAIR, B, PAIR), bf16),
            pltpu.VMEM((slots, length), f32),
            pltpu.VMEM((cols, length), bf16),
            pltpu.VMEM((cols, length), bf16),
            pltpu.VMEM((2 * cols, length), bf16),
            pltpu.VMEM((cols, length), f32),
            pltpu.VMEM((rows, cols, PAIR), bf16),
            pltpu.VMEM((slots, cols, PAIR), f32),
            pltpu.VMEM((slots + 1, cols, PAIR), f32),
            pltpu.VMEM((3, 2, n_row, cols, PAIR), bf16),
            pltpu.VMEM((3, 2, n_row, cols, PAIR), bf16),
            pltpu.VMEM((n_col, cols, length), bf16),
            pltpu.VMEM((n_row, piece, total_cols), sum_type),
            pltpu.VMEM((n_row, piece, total_cols), sum_type),
            pltpu.VMEM((piece, total_cols), sum_type),
            dma((tiles,)),
            dma((3, 2, n_row)), dma((3, 2, n_row)),
            dma((n_col,)), dma((n_col,)),
            dma((n_row,)), dma((n_row,)),
            dma((n_row,)), dma((n_row,)),
        ],
        compiler_params=pltpu.CompilerParams(
            collective_id=0, has_side_effects=True, vmem_limit_bytes=56 * 1024 * 1024
        ),
    )(send_rows, by_slot, holder, vectors, diagonal, upper)

    filtered, gram, projected = pl.pallas_call(
        functools.partial(output_kernel, cols),
        out_shape=(
            jax.ShapeDtypeStruct((cols, length), bf16),
            jax.ShapeDtypeStruct((cols, total_cols), f32),
            jax.ShapeDtypeStruct((cols, total_cols), f32),
        ),
        in_specs=[vmem, vmem],
        out_specs=(vmem, vmem, vmem),
    )(ordered, sums)
    return filtered, gram.T, projected.T


def solution(mesh):
    return jax.shard_map(
        on_device,
        mesh=mesh,
        in_specs=(P("col", "row"), P("row", None, None), P("row"), P("row", None), P("row")),
        out_specs=(P("col", "row"), P(None, "col"), P(None, "col")),
        check_vma=False,
    )
```

```python
import functools

import jax
import jax.numpy as jnp
from jax import lax
from jax.experimental import pallas as pl
from jax.experimental.pallas import tpu as pltpu
from jax.sharding import PartitionSpec as P

B = 64
K = 12
PAIR = 2 * B
TILE = 256
UNROLL = 16
ROWS_STEP = 16
HALF = B // 2

center_value = 0.25
half_width = 1.5

MESH = pl.DeviceIdType.MESH
NN = (((1,), (0,)), ((), ()))
NT = (((1,), (1,)), ((), ()))


def dot(a, b, dims):
    return lax.dot_general(a, b, dims, preferred_element_type=jnp.float32)


def order_matrix():
    row_at = lax.broadcasted_iota(jnp.int32, (TILE, TILE), 0)
    col_at = lax.broadcasted_iota(jnp.int32, (TILE, TILE), 1)
    within = row_at & (B - 1)
    target = (row_at - within) + (within & 1) * HALF + ((within >> 1) & 1) * (HALF // 2) + (within >> 2)
    return jnp.where(target == col_at, 1.0, 0.0).astype(jnp.bfloat16)


def build_kernel(rows, sources, counts, h, upper, diagonal, holder, order, swap, marks, placed, remote):
    step = pl.program_id(0)
    here = upper.shape[0]
    slots = remote.shape[0] - 1
    pieces = B * B // TILE
    first_row = step * here
    bf16 = jnp.bfloat16

    @pl.when(step == 0)
    def _():
        order[...] = order_matrix()
        row_at = lax.broadcasted_iota(jnp.int32, (TILE, TILE), 0)
        col_at = lax.broadcasted_iota(jnp.int32, (TILE, TILE), 1)
        swap[...] = jnp.where(col_at == (row_at & (pieces - 1)) * here + (row_at >> 4), 1.0, 0.0).astype(bf16)
        side = lax.broadcasted_iota(jnp.int32, (here, PAIR), 1) >> 6
        for wanted in range(3):
            marks[wanted] = jnp.where(side == wanted, 1.0, 0.0).astype(bf16)

    def clear_body(row, carry):
        upper[row] = jnp.zeros_like(upper[row])
        return carry

    lax.fori_loop(0, here, clear_body, 0)

    def order_body(pack, carry):
        for inner in range(2):
            slot = 2 * pack + inner
            lanes = jnp.concatenate([h[slot, :, at * TILE : (at + 1) * TILE] for at in range(pieces)], 0)
            swapped = dot(swap[...], lanes, NN).astype(bf16)
            value = dot(swapped, order[...], NN)
            for part in range(2):
                straight = value[:, part * PAIR : (part + 1) * PAIR]
                turned = pltpu.roll(straight, B, 1)
                placed[slot, 0, part] = straight.astype(bf16).reshape(here, pieces, PAIR)
                placed[slot, 1, part] = turned.astype(bf16).reshape(here, pieces, PAIR)
        return carry

    lax.fori_loop(0, K // 2, order_body, 0)

    def marked(slot, row, half, wanted):
        mark = marks[wanted]
        return jnp.concatenate(
            [placed[slot, turned, part, row] * mark for turned in (half, 1 - half) for part in range(2)], 0
        )

    def add_body(slot, carry):
        for group in range(here // UNROLL):
            news = []
            for row in range(group * UNROLL, (group + 1) * UNROLL):
                source = sources[slot, first_row + row]
                half = source & 1
                local = source < rows
                used = jnp.logical_and(slot < counts[first_row + row], local)
                pair = jnp.where(local, source >> 1, 0)
                new = upper[row, pair] + marked(slot, row, half, jnp.where(used, half, 2))
                news.append((row, pair, new))
            for row, pair, new in news:
                upper[row, pair] = new
        return carry

    lax.fori_loop(0, K, add_body, 0)

    def remote_body(group, carry):
        news = []
        for inner in range(4):
            row = 4 * group + inner
            for slot in (1, 2):
                source = sources[slot, first_row + row]
                at = jnp.where(source >= rows, source - rows, slots)
                holder[at] = first_row + row
                half = source & 1
                news.append((at, marked(slot, row, half, half)))
        for at, new in news:
            remote[at] = new
        return carry

    lax.fori_loop(0, here // 4, remote_body, 0)

    @pl.when(step == pl.num_programs(0) - 1)
    def _():
        diagonal[...] = jnp.zeros_like(diagonal)
        for slot in range(slots):
            part = slot % 4
            diagonal[slot // 4, pl.ds(part * B, B), pl.ds((part // 2) * PAIR, PAIR)] = remote[slot]


def output_kernel(cols, ordered, sums, filtered, gram, projected):
    order = order_matrix()
    for tile in range(ordered.shape[1] // TILE):
        here = pl.ds(tile * TILE, TILE)
        filtered[:, here] = dot(ordered[:, here], order, NT).astype(jnp.bfloat16)
    count, piece = sums.shape[0], sums.shape[1]
    for at in range(count):
        value = sums[at].astype(jnp.float32)
        first = at * piece
        if first < cols:
            gram[pl.ds(first, piece), :] = value
        else:
            projected[pl.ds(first - cols, piece), :] = value


def filter_kernel(
    n_row, n_col, send_rows, sources, holder, x_in, diagonal, dense_in,
    filtered, sum_in,
    dense, mask,
    x0, step_one, stacked, total, blocks, spread, upspread, out_buf, in_buf, gathered,
    piece_out, piece_in, sum_out,
    dense_sem,
    send_sem, recv_sem, col_send, col_recv, piece_send, piece_recv, sum_send, sum_recv,
):
    me = lax.axis_index("row")
    mine = lax.axis_index("col")
    cols, length = x_in.shape
    rows = length // B
    pairs = length // PAIR
    slots = 2 * n_row
    tiles = length // TILE
    per_tile = TILE // B
    bf16 = jnp.bfloat16
    f32 = jnp.float32

    barrier = pltpu.get_barrier_semaphore()
    for step in range(1, n_row):
        pl.semaphore_signal(barrier, inc=1, device_id={"row": lax.rem(me + step, n_row)}, device_id_type=MESH)
    for step in range(1, n_col):
        pl.semaphore_signal(barrier, inc=1, device_id={"col": lax.rem(mine + step, n_col)}, device_id_type=MESH)

    def dense_copy(tile):
        here = pl.ds(tile * per_tile, per_tile)
        return pltpu.make_async_copy(
            dense_in.at[here], dense.at[here], dense_sem.at[tile]
        )

    for tile in range(tiles):
        dense_copy(tile).start()

    def columns(at, width):
        return pl.ds(pl.multiple_of(at * width, width), width)

    low = lax.broadcasted_iota(jnp.int32, (cols, PAIR), 1) < B

    def both(values):
        turned = pltpu.roll(values, B, 1)
        return jnp.where(low, values, turned), jnp.where(low, turned, values)

    lane_block = lax.broadcasted_iota(jnp.int32, (1, length), 1) >> 6

    def mask_body(slot, carry):
        mask[pl.ds(slot, 1), :] = jnp.where(lane_block == send_rows[slot], 1.0, 0.0)
        return carry

    lax.fori_loop(0, slots, mask_body, 0)

    def keep_blocks(pair, values):
        first, second = both(values)
        blocks[2 * pair] = first.astype(bf16)
        blocks[2 * pair + 1] = second.astype(bf16)

    order = order_matrix()
    for tile in range(tiles):
        here = pl.ds(tile * TILE, TILE)
        value = dot(x_in[:, here], order, NN)
        x0[:, here] = value.astype(bf16)
        keep_blocks(2 * tile, value[:, :PAIR])
        keep_blocks(2 * tile + 1, value[:, PAIR:])

    upspread[slots] = jnp.zeros((cols, PAIR), f32)

    def arrived_at(row, slot):
        source = sources[slot, row]
        return upspread[jnp.where(source >= rows, source - rows, slots)]

    pl.semaphore_wait(barrier, n_row + n_col - 2)

    def row_copy(phase, kind, slot_here, slot_there, peer):
        return pltpu.make_async_remote_copy(
            src_ref=out_buf.at[phase, kind, slot_here],
            dst_ref=in_buf.at[phase, kind, slot_there],
            send_sem=send_sem.at[phase, kind, slot_here],
            recv_sem=recv_sem.at[phase, kind, slot_there],
            device_id={"row": peer},
            device_id_type=MESH,
        )

    def send_all(phase, kind):
        for step in range(1, n_row):
            peer = lax.rem(me + step, n_row)
            row_copy(phase, kind, peer, me, peer).start()
        in_buf[phase, kind, me] = out_buf[phase, kind, me]

    def wait_all(phase, kind):
        for step in range(1, n_row):
            peer = lax.rem(me + step, n_row)
            row_copy(phase, kind, peer, peer, peer).wait_recv()

    def pick(first, second):
        return jnp.where(low, blocks[first].astype(f32), blocks[second].astype(f32)).astype(bf16)

    def apply_operator(phase, source, finish, beside=None):
        for peer in range(n_row):
            out_buf[phase, 0, peer] = pick(send_rows[2 * peer], send_rows[2 * peer + 1])
        send_all(phase, 0)
        for pack in range(slots // 4):
            at = 4 * pack
            near = jnp.concatenate([pick(holder[at], holder[at + 1]), pick(holder[at + 2], holder[at + 3])], 1)
            product = dot(near, diagonal[pack], NN).astype(bf16)
            for inner in range(2):
                out_buf[phase, 1, 2 * pack + inner] = product[:, inner * PAIR : (inner + 1) * PAIR]
        send_all(phase, 1)

        def local_body(tile, carry):
            down = jnp.concatenate([dense[:, 2 * tile + side].reshape(length, PAIR) for side in range(2)], 1)
            along = jnp.concatenate(
                [dense[pl.ds(tile * per_tile, per_tile), pair].reshape(TILE, PAIR) for pair in range(pairs)], 1
            )
            total[:, columns(tile, TILE)] = dot(source[...], down, NN) + dot(source[...], along, NT)
            return carry

        if phase == 0:
            for tile in range(tiles):
                dense_copy(tile).wait()

        lax.fori_loop(0, tiles, local_body, 0)
        wait_all(phase, 0)
        for pack in range(slots // 4):
            far = jnp.concatenate([in_buf[phase, 0, 2 * pack + inner] for inner in range(2)], 1)
            product = dot(far, diagonal[pack], NT)
            for inner in range(2):
                peer = 2 * pack + inner
                first, second = both(product[:, inner * PAIR : (inner + 1) * PAIR])
                upspread[2 * peer] = first
                upspread[2 * peer + 1] = second
        wait_all(phase, 1)
        for peer in range(n_row):
            first, second = both(in_buf[phase, 1, peer].astype(f32))
            spread[2 * peer] = first
            spread[2 * peer + 1] = second
        if beside is not None:
            beside()

        def finish_body(pair, carry):
            here = columns(pair, PAIR)
            value = total[:, here] + jnp.where(
                low,
                arrived_at(2 * pair, 1) + arrived_at(2 * pair, 2),
                arrived_at(2 * pair + 1, 1) + arrived_at(2 * pair + 1, 2),
            )
            for slot in range(slots):
                value = value + spread[slot] * mask[pl.ds(slot, 1), here]
            finish(pair, here, value)
            return carry

        lax.fori_loop(0, pairs, finish_body, 0)

    def first_finish(pair, here, value):
        new = ((value - center_value * x0[:, here].astype(f32)) / half_width).astype(bf16)
        step_one[:, here] = new
        keep_blocks(pair, new.astype(f32))

    def second_finish(pair, here, value):
        old = step_one[:, here].astype(f32)
        new = (2.0 * (value - center_value * old) / half_width - x0[:, here].astype(f32)).astype(bf16)
        stacked[pl.ds(0, cols), here] = new
        gathered[mine, :, here] = new
        filtered[:, here] = new
        keep_blocks(pair, new.astype(f32))

    def third_finish(pair, here, value):
        stacked[pl.ds(cols, cols), here] = value.astype(bf16)

    def col_copy(slot_here, slot_there, sem_at, peer):
        return pltpu.make_async_remote_copy(
            src_ref=gathered.at[slot_here],
            dst_ref=gathered.at[slot_there],
            send_sem=col_send.at[sem_at],
            recv_sem=col_recv.at[slot_there],
            device_id={"col": peer},
            device_id_type=MESH,
        )

    sibling = mine + 1 - 2 * lax.rem(mine, 2)
    across = [lax.rem(mine + 2 * step, n_col) for step in range(1, n_col // 2)]

    def start_gather():
        for at, peer in enumerate(across):
            col_copy(mine, mine, at, peer).start()
        col_copy(mine, mine, len(across), sibling).start()

    def forward_gather():
        for at, peer in enumerate(across):
            col_copy(peer, peer, at, peer).wait_recv()
            col_copy(peer, peer, len(across) + 1 + at, sibling).start()

    def end_gather():
        col_copy(sibling, sibling, 0, sibling).wait_recv()
        for peer in across:
            other = peer + 1 - 2 * lax.rem(peer, 2)
            col_copy(other, other, 0, sibling).wait_recv()

    apply_operator(0, x0, first_finish)
    apply_operator(1, step_one, second_finish)
    start_gather()
    apply_operator(2, stacked.at[pl.ds(0, cols)], third_finish, forward_gather)
    end_gather()

    piece = 2 * cols // n_row
    part = dot(stacked[...], gathered[...].reshape(n_col * cols, length), NT)
    for at in range(n_row):
        piece_out[at] = part[at * piece : (at + 1) * piece].astype(piece_out.dtype)

    def piece_copy(slot_here, slot_there, peer):
        return pltpu.make_async_remote_copy(
            src_ref=piece_out.at[slot_here],
            dst_ref=piece_in.at[slot_there],
            send_sem=piece_send.at[slot_here],
            recv_sem=piece_recv.at[slot_there],
            device_id={"row": peer},
            device_id_type=MESH,
        )

    def sum_copy(slot_there, peer):
        return pltpu.make_async_remote_copy(
            src_ref=sum_out,
            dst_ref=sum_in.at[slot_there],
            send_sem=sum_send.at[peer],
            recv_sem=sum_recv.at[slot_there],
            device_id={"row": peer},
            device_id_type=MESH,
        )

    peers = [lax.rem(me + step, n_row) for step in range(1, n_row)]
    for peer in peers:
        piece_copy(peer, me, peer).start()
    piece_in[me] = piece_out[me]
    for peer in peers:
        piece_copy(peer, peer, peer).wait_recv()
    summed = piece_in[0].astype(f32)
    for peer in range(1, n_row):
        summed = summed + piece_in[peer].astype(f32)
    sum_out[...] = summed.astype(sum_out.dtype)
    for peer in peers:
        sum_copy(me, peer).start()
    sum_in[me] = sum_out[...]
    for peer in peers:
        sum_copy(peer, peer).wait_recv()
    for peer in peers:
        for phase in range(3):
            row_copy(phase, 0, peer, me, peer).wait_send()
            row_copy(phase, 1, peer, me, peer).wait_send()
        piece_copy(peer, me, peer).wait_send()
        sum_copy(me, peer).wait_send()
    for at, peer in enumerate(across):
        col_copy(mine, mine, at, peer).wait_send()
        col_copy(peer, peer, len(across) + 1 + at, sibling).wait_send()
    col_copy(mine, mine, len(across), sibling).wait_send()


def on_device(vectors, hblocks, counts, sources, send_rows):
    rows = hblocks.shape[0]
    cols, length = vectors.shape
    slots = send_rows.shape[0]
    n_row = lax.axis_size("row")
    n_col = lax.axis_size("col")
    assert slots == 2 * n_row
    tiles = length // TILE
    total_cols = n_col * cols
    piece = 2 * cols // n_row
    sum_type = jnp.bfloat16 if piece % 16 == 0 else jnp.float32
    smem = pl.BlockSpec(memory_space=pltpu.SMEM)
    vmem = pl.BlockSpec(memory_space=pltpu.VMEM)
    dma = pltpu.SemaphoreType.DMA
    bf16 = jnp.bfloat16
    f32 = jnp.float32
    by_slot = sources.T
    upper, diagonal, holder = pl.pallas_call(
        functools.partial(build_kernel, rows),
        grid=(rows // ROWS_STEP,),
        out_shape=(
            jax.ShapeDtypeStruct((rows, rows // 2, B, PAIR), bf16),
            jax.ShapeDtypeStruct((slots // 4, TILE, TILE), bf16),
            jax.ShapeDtypeStruct((slots + 1,), jnp.int32),
        ),
        in_specs=[smem, smem, pl.BlockSpec((K, ROWS_STEP, B * B), lambda step: (0, step, 0))],
        out_specs=(
            pl.BlockSpec((ROWS_STEP, rows // 2, B, PAIR), lambda step: (step, 0, 0, 0)),
            pl.BlockSpec((slots // 4, TILE, TILE), lambda step: (0, 0, 0)),
            smem,
        ),
        scratch_shapes=[
            pltpu.VMEM((TILE, TILE), bf16),
            pltpu.VMEM((TILE, TILE), bf16),
            pltpu.VMEM((3, ROWS_STEP, PAIR), bf16),
            pltpu.VMEM((K, 2, 2, ROWS_STEP, B * B // TILE, PAIR), bf16),
            pltpu.VMEM((slots + 1, B, PAIR), bf16),
        ],
        compiler_params=pltpu.CompilerParams(vmem_limit_bytes=56 * 1024 * 1024),
    )(by_slot, counts, hblocks.transpose(1, 0, 2))

    ordered, sums = pl.pallas_call(
        functools.partial(filter_kernel, n_row, n_col),
        out_shape=(
            jax.ShapeDtypeStruct((cols, length), bf16),
            jax.ShapeDtypeStruct((n_row, piece, total_cols), sum_type),
        ),
        in_specs=[smem, smem, smem, vmem, vmem, pl.BlockSpec(memory_space=pl.ANY)],
        out_specs=(vmem, vmem),
        scratch_shapes=[
            pltpu.VMEM((rows, length // PAIR, B, PAIR), bf16),
            pltpu.VMEM((slots, length), f32),
            pltpu.VMEM((cols, length), bf16),
            pltpu.VMEM((cols, length), bf16),
            pltpu.VMEM((2 * cols, length), bf16),
            pltpu.VMEM((cols, length), f32),
            pltpu.VMEM((rows, cols, PAIR), bf16),
            pltpu.VMEM((slots, cols, PAIR), f32),
            pltpu.VMEM((slots + 1, cols, PAIR), f32),
            pltpu.VMEM((3, 2, n_row, cols, PAIR), bf16),
            pltpu.VMEM((3, 2, n_row, cols, PAIR), bf16),
            pltpu.VMEM((n_col, cols, length), bf16),
            pltpu.VMEM((n_row, piece, total_cols), sum_type),
            pltpu.VMEM((n_row, piece, total_cols), sum_type),
            pltpu.VMEM((piece, total_cols), sum_type),
            dma((tiles,)),
            dma((3, 2, n_row)), dma((3, 2, n_row)),
            dma((n_col,)), dma((n_col,)),
            dma((n_row,)), dma((n_row,)),
            dma((n_row,)), dma((n_row,)),
        ],
        compiler_params=pltpu.CompilerParams(
            collective_id=0, has_side_effects=True, vmem_limit_bytes=56 * 1024 * 1024
        ),
    )(send_rows, by_slot, holder, vectors, diagonal, upper)

    filtered, gram, projected = pl.pallas_call(
        functools.partial(output_kernel, cols),
        out_shape=(
            jax.ShapeDtypeStruct((cols, length), bf16),
            jax.ShapeDtypeStruct((cols, total_cols), f32),
            jax.ShapeDtypeStruct((cols, total_cols), f32),
        ),
        in_specs=[vmem, vmem],
        out_specs=(vmem, vmem, vmem),
    )(ordered, sums)
    return filtered, gram.T, projected.T


def solution(mesh):
    return jax.shard_map(
        on_device,
        mesh=mesh,
        in_specs=(P("col", "row"), P("row", None, None), P("row"), P("row", None), P("row")),
        out_specs=(P("col", "row"), P(None, "col"), P(None, "col")),
        check_vma=False,
    )
```
